128 devices in a mesh: group: 4 (over z), dev: 32 (over x, y, core).
Axes of the slice: x: 4, y: 4, z: 4, core: 2. Of those that a mesh axis runs over, the one named last changes fastest.
Arguments:
- populations: float32 [512, 19, 4096], P(('group', 'dev')), may hold values from -3 to 3
- fluid_flags: int32 [512, 4096], P(('group', 'dev')), may hold values from 0 to 1, as said below
- neighbours: int32 [512, 18], P(('group', 'dev')), may hold values from -1 to 11, as said below
- relax_rate: float32 [512], P(('group', 'dev')), may hold values from 1 to 1.9
Outputs:
- advanced: float32 [512, 19, 4096], P(('group', 'dev'))
The draws below stay inside these ranges and needn't reach their ends.
Inputs may be any that keep to these rules, and one draw needn't show every extreme that they name: `fluid_flags`: on every device the slots that hold a block come first and the later slots have no fluid cell. In every group some device holds a block in all 4 slots. `neighbours`: an entry is -1 or (dz + 1) * 4 + t, where dz is the third component of the direction; it names slot t of the device dz places further along dev in the same group, a slot that holds a block, and that block's entry in the opposite direction names back. Slots that hold no block have -1 in every direction.
All inputs are finite; a program needn't handle non-finite values.
Results may differ from the reference program's by a relative error of at most 0.0003.
Values sent between devices are 32-bit elements; how exact they have to be, the bound alone decides.
A program may use at most 128 MiB of HBM per device.

```python
import jax
import jax.numpy as jnp
import numpy as np
from jax import lax

BLOCK = 16
PX = 4
PY = 1
STEPS = 2
SLOTS = 4
CELLS = 4096
NBLOCKS = 512
N_GROUP = 4
N_DEV = 32


def directions():
    listed = []
    for axis_num in range(3):
        for side_sign in (1, -1):
            vector = [0, 0, 0]
            vector[axis_num] = side_sign
            listed.append(vector)
    for axis_one, axis_two in ((0, 1), (0, 2), (1, 2)):
        for sign_one in (1, -1):
            for sign_two in (1, -1):
                vector = [0, 0, 0]
                vector[axis_one] = sign_one
                vector[axis_two] = sign_two
                listed.append(vector)
    return np.array(listed, dtype=np.int32)


def geometry(key):
    device_count = N_GROUP * N_DEV
    slot_count = PX * PY
    subkeys = jax.random.split(jax.random.fold_in(key, 11), 5)
    light_load = jax.random.randint(subkeys[0], (device_count,), slot_count // 4, slot_count // 2 + 1)
    heavy_pick = jax.random.randint(subkeys[1], (N_GROUP,), 0, N_DEV)
    extra_heavy = jax.random.randint(subkeys[2], (device_count,), 0, 8) == 0
    device_ids = jnp.arange(device_count)
    heavy_dev = (device_ids % N_DEV == heavy_pick[device_ids // N_DEV]) | extra_heavy
    live_slots = jnp.where(heavy_dev, slot_count, light_load)
    orders = jax.vmap(lambda subkey: jax.random.permutation(subkey, slot_count))(jax.random.split(subkeys[3], device_count))
    holder = jnp.argsort(orders, axis=1)
    return (live_slots, orders, holder, subkeys[4])


def draw_fluid_flags(key, part):
    device_count = N_GROUP * N_DEV
    slot_count = PX * PY
    live_slots, orders, holder, cell_key = geometry(key)
    wet_draw = jax.random.randint(cell_key, (device_count, slot_count, BLOCK ** 3), 0, 20) < 17
    holds = jnp.arange(slot_count)[None, :] < live_slots[:, None]
    return (wet_draw & holds[:, :, None]).astype(jnp.int32).reshape(device_count * slot_count, BLOCK ** 3)


def draw_neighbours(key, part):
    device_count = N_GROUP * N_DEV
    slot_count = PX * PY
    live_slots, orders, holder, cell_key = geometry(key)
    offsets = jnp.asarray(directions())
    pos_x = orders // PY
    pos_y = orders % PY
    to_x = pos_x[:, :, None] + offsets[None, None, :, 0]
    to_y = pos_y[:, :, None] + offsets[None, None, :, 1]
    device_ids = jnp.arange(device_count)
    along_dev = (device_ids % N_DEV)[:, None, None] + offsets[None, None, :, 2]
    inside = (to_x >= 0) & (to_x < PX) & (to_y >= 0) & (to_y < PY) & (along_dev >= 0) & (along_dev < N_DEV)
    to_dev = jnp.clip(device_ids[:, None, None] + offsets[None, None, :, 2], 0, device_count - 1)
    to_pos = jnp.clip(to_x, 0, PX - 1) * PY + jnp.clip(to_y, 0, PY - 1)
    to_slot = holder[to_dev, to_pos]
    own_live = jnp.arange(slot_count)[None, :, None] < live_slots[:, None, None]
    present = inside & (to_slot < live_slots[to_dev]) & own_live
    entries = jnp.where(present, (offsets[None, None, :, 2] + 1) * slot_count + to_slot, -1)
    return entries.reshape(device_count * slot_count, 18).astype(jnp.int32)


def levels(stream_key, shape, cuts, least, top_value):
    loudness = 1.0
    for position, parts in cuts:
        draws = jax.random.uniform(jax.random.fold_in(jax.random.fold_in(stream_key, 6), position), (parts,), jnp.float32, least / len(cuts), top_value / len(cuts))
        loudness = loudness * jnp.repeat(jnp.exp(draws), shape[position] // parts).reshape((-1,) + (1,) * (len(shape) - 1 - position))
    return loudness


def gaussian(key, shape, deviation, bound, cuts=(), kind=jnp.bfloat16):
    values = deviation * jax.random.normal(key, shape, jnp.float32)
    if cuts:
        values = values * levels(key, shape, cuts, -0.22, 0.18)
    return jnp.clip(values, -bound, bound).astype(kind)


def setup_inputs(seed: int = 0) -> dict:
    arg_keys = jax.random.split(jax.random.key(seed), 5)
    populations = gaussian(arg_keys[0], (NBLOCKS, 19, CELLS), 0.5, 3.0, ((0, 128),), jnp.float32)
    fluid_flags = draw_fluid_flags(jax.random.fold_in(arg_keys[4], 71), 0)
    neighbours = draw_neighbours(jax.random.fold_in(arg_keys[4], 71), 0)
    relax_rate = jnp.clip(1.0 + 0.9 * jax.random.uniform(arg_keys[3], (NBLOCKS,), jnp.float32) ** levels(arg_keys[3], (NBLOCKS,), ((0, 128),), -0.2, 0.2), 1.0, 1.9)
    return {"populations": populations, "fluid_flags": fluid_flags, "neighbours": neighbours, "relax_rate": relax_rate}


def invert_matrix(rows_in):
    size_n = len(rows_in)
    work = [list(rows_in[row_num]) + [1.0 if col_num == row_num else 0.0 for col_num in range(size_n)] for row_num in range(size_n)]
    for col_num in range(size_n):
        pivot_row = max(range(col_num, size_n), key=lambda row_num: abs(work[row_num][col_num]))
        work[col_num], work[pivot_row] = work[pivot_row], work[col_num]
        pivot_val = work[col_num][col_num]
        work[col_num] = [entry / pivot_val for entry in work[col_num]]
        for row_num in range(size_n):
            if row_num != col_num:
                factor = work[row_num][col_num]
                if factor != 0.0:
                    work[row_num] = [entry - factor * pivot_entry for entry, pivot_entry in zip(work[row_num], work[col_num])]
    return [row_list[size_n:] for row_list in work]


def lattice():
    velocity = [[0, 0, 0]]
    for axis_num in range(3):
        for side_sign in (1, -1):
            vector = [0, 0, 0]
            vector[axis_num] = side_sign
            velocity.append(vector)
    for axis_one, axis_two in ((0, 1), (0, 2), (1, 2)):
        for sign_one in (1, -1):
            for sign_two in (1, -1):
                vector = [0, 0, 0]
                vector[axis_one] = sign_one
                vector[axis_two] = sign_two
                velocity.append(vector)
    weights = [1.0 / 3.0] + [1.0 / 18.0] * 6 + [1.0 / 36.0] * 12
    opposite = [velocity.index([-entry for entry in velocity[lane_num]]) for lane_num in range(19)]
    comp_x = [float(vector[0]) for vector in velocity]
    comp_y = [float(vector[1]) for vector in velocity]
    comp_z = [float(vector[2]) for vector in velocity]
    makers = [
        lambda a, b, c: 1.0, lambda a, b, c: a, lambda a, b, c: b, lambda a, b, c: c,
        lambda a, b, c: a * b, lambda a, b, c: a * c, lambda a, b, c: b * c,
        lambda a, b, c: a * a - b * b, lambda a, b, c: a * a - c * c, lambda a, b, c: a * a + b * b + c * c,
        lambda a, b, c: a * b * b, lambda a, b, c: a * c * c, lambda a, b, c: b * a * a, lambda a, b, c: b * c * c,
        lambda a, b, c: c * a * a, lambda a, b, c: c * b * b, lambda a, b, c: a * a * b * b,
        lambda a, b, c: a * a * c * c, lambda a, b, c: b * b * c * c]
    moment_rows = [[maker(comp_x[col_num], comp_y[col_num], comp_z[col_num]) for col_num in range(19)] for maker in makers]
    inverse = invert_matrix(moment_rows)
    table_other = []
    table_shear = []
    for row_num in range(19):
        other_row = []
        shear_row = []
        for col_num in range(19):
            other_sum = sum(inverse[row_num][mom_num] * moment_rows[mom_num][col_num] for mom_num in range(9, 19))
            shear_sum = sum(inverse[row_num][mom_num] * moment_rows[mom_num][col_num] for mom_num in range(4, 9))
            ratio = weights[col_num] / weights[row_num]
            other_row.append(other_sum * ratio)
            shear_row.append(shear_sum * ratio)
        table_other.append(other_row)
        table_shear.append(shear_row)
    return np.array(velocity), np.array(weights), opposite, np.array(table_other), np.array(table_shear)


def collide(current, rates):
    velocity, weights, opposite, table_other, table_shear = lattice()
    moment_in = np.concatenate([weights[None, :], (weights[:, None] * velocity).T], 0)
    density_momentum = jnp.einsum("ki,nic->nkc", jnp.asarray(moment_in, jnp.float32), current, precision=lax.Precision.HIGHEST)
    density = density_momentum[:, 0]
    momentum = density_momentum[:, 1:]
    projected = jnp.einsum("ik,nkc->nic", jnp.asarray(velocity, jnp.float32), momentum, precision=lax.Precision.HIGHEST)
    speed_sq = jnp.sum(momentum * momentum, axis=1)
    equilibrium = density[:, None] + 3.0 * projected + 4.5 * projected * projected - 1.5 * speed_sq[:, None]
    departure = current - equilibrium
    matrices = jnp.asarray(table_other, jnp.float32)[None] + rates[:, None, None] * jnp.asarray(table_shear, jnp.float32)[None]
    return current - jnp.einsum("nij,njc->nic", matrices, departure, precision=lax.Precision.HIGHEST)


def make_slabs(collided, fluid_flags):
    velocity = lattice()[0]
    block_count = collided.shape[0]
    blocked = collided.reshape(block_count, 19, BLOCK, BLOCK, BLOCK)
    wet_cells = fluid_flags.reshape(block_count, BLOCK, BLOCK, BLOCK).astype(jnp.float32)
    face_list = []
    for lane_num in range(1, 7):
        axis_num = int(np.argmax(np.abs(velocity[lane_num])))
        side_sign = int(velocity[lane_num][axis_num])
        layer_index = BLOCK - 1 if side_sign > 0 else 0
        members = [lane_two for lane_two in range(19) if int(velocity[lane_two][axis_num]) == side_sign]
        layer_values = lax.index_in_dim(blocked, layer_index, axis_num + 2, keepdims=False)[:, members]
        layer_flags = lax.index_in_dim(wet_cells, layer_index, axis_num + 1, keepdims=False)
        face_list.append(jnp.concatenate([layer_values, layer_flags[:, None]], 1).reshape(block_count, 6, BLOCK * BLOCK))
    edge_list = []
    for lane_num in range(7, 19):
        nonzero = [axis_num for axis_num in range(3) if int(velocity[lane_num][axis_num]) != 0]
        axis_one, axis_two = nonzero
        end_one = BLOCK - 1 if velocity[lane_num][axis_one] > 0 else 0
        end_two = BLOCK - 1 if velocity[lane_num][axis_two] > 0 else 0
        line_values = lax.index_in_dim(lax.index_in_dim(blocked[:, lane_num], end_one, axis_one + 1, keepdims=False), end_two, axis_two, keepdims=False)
        line_flags = lax.index_in_dim(lax.index_in_dim(wet_cells, end_one, axis_one + 1, keepdims=False), end_two, axis_two, keepdims=False)
        edge_list.append(jnp.stack([line_values, line_flags], 1))
    return jnp.stack(face_list, 1), jnp.stack(edge_list, 1)


def propagate(current, collided, fluid_flags, rim_faces, rim_edges):
    velocity, weights, opposite, table_other, table_shear = lattice()
    block_count = current.shape[0]
    blocked = collided.reshape(block_count, 19, BLOCK, BLOCK, BLOCK)
    wet_cells = fluid_flags.reshape(block_count, BLOCK, BLOCK, BLOCK).astype(jnp.float32)
    padded = jnp.zeros((block_count, 19, BLOCK + 2, BLOCK + 2, BLOCK + 2), collided.dtype)
    padded = padded.at[:, :, 1:-1, 1:-1, 1:-1].set(blocked)
    open_mask = jnp.zeros((block_count, BLOCK + 2, BLOCK + 2, BLOCK + 2), wet_cells.dtype)
    open_mask = open_mask.at[:, 1:-1, 1:-1, 1:-1].set(wet_cells)
    inner = slice(1, BLOCK + 1)
    for face_num in range(6):
        lane_num = face_num + 1
        axis_num = int(np.argmax(np.abs(velocity[lane_num])))
        side_sign = int(velocity[lane_num][axis_num])
        rim_at = BLOCK + 1 if side_sign > 0 else 0
        spatial = tuple(rim_at if axis_two == axis_num else inner for axis_two in range(3))
        members = [lane_two for lane_two in range(19) if int(velocity[lane_two][axis_num]) == -side_sign]
        face_values = rim_faces[:, face_num].reshape(block_count, 6, BLOCK, BLOCK)
        for member_num, lane_two in enumerate(members):
            padded = padded.at[(slice(None), lane_two) + spatial].set(face_values[:, member_num])
        open_mask = open_mask.at[(slice(None),) + spatial].set(face_values[:, 5])
    for edge_num in range(12):
        lane_num = edge_num + 7
        spatial = tuple((BLOCK + 1 if velocity[lane_num][axis_two] > 0 else 0) if int(velocity[lane_num][axis_two]) != 0 else inner for axis_two in range(3))
        padded = padded.at[(slice(None), opposite[lane_num]) + spatial].set(rim_edges[:, edge_num, 0])
        open_mask = open_mask.at[(slice(None),) + spatial].set(rim_edges[:, edge_num, 1])
    arrived_list = []
    for lane_num in range(19):
        window = tuple(slice(1 - int(component), 1 - int(component) + BLOCK) for component in velocity[lane_num])
        pulled = padded[(slice(None), lane_num) + window]
        open_here = open_mask[(slice(None),) + window]
        arrived_list.append(jnp.where(open_here > 0, pulled, blocked[:, opposite[lane_num]]))
    arrived = jnp.stack(arrived_list, 1).reshape(block_count, 19, BLOCK * BLOCK * BLOCK)
    return jnp.where(fluid_flags[:, None, :] > 0, arrived, current)


def reference(populations, fluid_flags, neighbours, relax_rate):
    device_count = N_GROUP * N_DEV
    current = populations
    flags_split = fluid_flags.reshape(device_count, SLOTS, CELLS)
    table_split = neighbours.reshape(device_count, SLOTS, 18)
    rates_split = relax_rate.reshape(device_count, SLOTS)
    for step_num in range(STEPS):
        def slab_share(packed):
            share_pops, share_flags, share_rates = packed
            return make_slabs(collide(share_pops, share_rates), share_flags)

        face_slabs, edge_slabs = lax.map(slab_share, (current.reshape(device_count, SLOTS, 19, CELLS), flags_split, rates_split))
        face_slabs = face_slabs.reshape((NBLOCKS,) + face_slabs.shape[2:])
        edge_slabs = edge_slabs.reshape((NBLOCKS,) + edge_slabs.shape[2:])

        def advance(packed):
            share_pops, share_flags, share_table, share_rates, device_num = packed
            collided = collide(share_pops, share_rates)
            present = share_table >= 0
            global_id = jnp.where(present, (device_num + share_table // SLOTS - 1) * SLOTS + share_table % SLOTS, 0)
            rim_faces = jnp.stack([jnp.where(present[:, face_num, None, None], face_slabs[global_id[:, face_num], face_num ^ 1], 0.0) for face_num in range(6)], 1)
            rim_edges = jnp.stack([jnp.where(present[:, 6 + edge_num, None, None], edge_slabs[global_id[:, 6 + edge_num], 4 * (edge_num // 4) + 3 - edge_num % 4], 0.0) for edge_num in range(12)], 1)
            return propagate(share_pops, collided, share_flags, rim_faces, rim_edges)

        current = lax.map(advance, (current.reshape(device_count, SLOTS, 19, CELLS), flags_split, table_split, rates_split, jnp.arange(device_count, dtype=jnp.int32)))
        current = current.reshape(NBLOCKS, 19, CELLS)
    return current
```

```python
import functools

import jax
import jax.numpy as jnp
import numpy as np
from jax import lax
from jax.experimental import pallas as pl
from jax.experimental.pallas import tpu as pltpu
from jax.sharding import PartitionSpec as P

SLOTS = 4
CELLS = 4096
LANES = 128
MESH = pl.DeviceIdType.MESH
CLOSED = np.float32(np.inf)


def velocities():
    found = [(0, 0, 0)]
    for axis in range(3):
        for sign in (1, -1):
            v = [0, 0, 0]
            v[axis] = sign
            found.append(tuple(v))
    for one, two in ((0, 1), (0, 2), (1, 2)):
        for sign_one in (1, -1):
            for sign_two in (1, -1):
                v = [0, 0, 0]
                v[one] = sign_one
                v[two] = sign_two
                found.append(tuple(v))
    return found


VEL = velocities()
OPP = [VEL.index(tuple(-c for c in v)) for v in VEL]
UP = [i for i, v in enumerate(VEL) if v[2] == 1]
DOWN = [i for i, v in enumerate(VEL) if v[2] == -1]

def column(direction):
    return VEL.index(direction) - 1


def collide(g, rate):
    sx, dx = g[1] + g[2], g[1] - g[2]
    sy, dy = g[3] + g[4], g[3] - g[4]
    sz, dz = g[5] + g[6], g[5] - g[6]

    def plane(first):
        a, b = g[first] + g[first + 3], g[first + 1] + g[first + 2]
        c, d = g[first] - g[first + 3], g[first + 1] - g[first + 2]
        return a + b, a - b, c + d, c - d

    exy, qxy, x1, y1 = plane(7)
    exz, qxz, x2, z1 = plane(11)
    eyz, qyz, y2, z2 = plane(15)
    sixth = np.float32(1 / 6)
    ux = (dx + 0.5 * (x1 + x2)) * sixth
    uy = (dy + 0.5 * (y1 + y2)) * sixth
    uz = (dz + 0.5 * (z1 + z2)) * sixth
    xx = (sx + sx) + (exy + exz)
    yy = (sy + sy) + (exy + eyz)
    zz = (sz + sz) + (exz + eyz)
    total = xx + yy + zz
    edges = exy + exz + eyz
    density = g[0] * np.float32(1 / 3) + (total - edges) * np.float32(1 / 36)
    ux2, uy2, uz2 = ux * ux, uy * uy, uz * uz
    u2 = ux2 + uy2 + uz2
    keep = 1.0 - rate
    quarter = 0.25 * keep
    base = density - u2 * sixth
    face = base + (keep * np.float32(1 / 3)) * u2 - (quarter * np.float32(1 / 3)) * total
    half_less = 0.5 - keep
    out = [None] * 19
    out[0] = base
    for first, along, u, square in ((1, xx, ux, ux2), (3, yy, uy, uy2), (5, zz, uz, uz2)):
        even = face + quarter * along + half_less * square
        out[first], out[first + 1] = even + u, even - u
    hx, hy, hz = 0.5 * ux2, 0.5 * uy2, 0.5 * uz2
    for first, ua, ub, ha, hb, q in (
        (7, ux, uy, hx, hy, qxy),
        (11, ux, uz, hx, hz, qxz),
        (15, uy, uz, hy, hz, qyz),
    ):
        cross = rate * (ua * ub) + quarter * q
        even = base + (ha + hb)
        plus, minus = even + cross, even - cross
        add, sub = ua + ub, ua - ub
        out[first], out[first + 3] = plus + add, plus - add
        out[first + 1], out[first + 2] = minus + sub, minus - sub
    return out


def roll(v, shift):
    shift = shift % LANES
    return v if shift == 0 else pltpu.roll(v, shift, 1)


def kernel(
    n_dev,
    x_hbm,
    flags_hbm,
    near_hbm,
    rate_ref,
    out_ref,
    x_ref,
    flags_ref,
    near_ref,
    c1_ref,
    c2_ref,
    g1_ref,
    index_ref,
    present_ref,
    fsend,
    fland,
    send1,
    send2,
    land1,
    land2,
    rim_ref,
    rim_y_ref,
    in_sem,
    small_sem,
    fsend_sem,
    frecv_sem,
    send_sem,
    recv_sem,
):
    me = lax.axis_index("dev")
    above, below = lax.rem(me + 1, n_dev), lax.rem(me + n_dev - 1, n_dev)
    to = (above, below)

    barrier = pltpu.get_barrier_semaphore()
    for other in to:
        pl.semaphore_signal(barrier, inc=1, device_id={"dev": other}, device_id_type=MESH)

    def fetch(r):
        part = pl.ds(r * 4, 4)
        return pltpu.make_async_copy(x_hbm.at[:, part], x_ref.at[:, part], in_sem.at[r])

    fetch_flags = pltpu.make_async_copy(flags_hbm, flags_ref, small_sem.at[0])
    fetch_near = pltpu.make_async_copy(near_hbm, near_ref, small_sem.at[1])
    fetch_flags.start()
    fetch_near.start()
    for r in range(4):
        fetch(r).start()

    lane = lax.broadcasted_iota(jnp.int32, (8, LANES), 1)
    row = lax.broadcasted_iota(jnp.int32, (8, LANES), 0)
    z = lane & 15
    z_rim = {1: z == 0, -1: z == 15}
    y_rim = {1: lane >= 112, -1: lane < 16}
    half = row >> 2

    rate = jnp.full((8, LANES), rate_ref[0], jnp.float32)
    for s in range(1, SLOTS):
        rate = jnp.where((row & 3) == s, rate_ref[s], rate)

    fetch_flags.wait()

    def pack_flags(q, _):
        pair = [(flags_ref[2 * q + k] > 0).astype(jnp.float32) for k in range(2)]
        up = jnp.where(z == 7, roll(pair[0], -8), 0.0) + jnp.where(z == 15, pair[1], 0.0)
        down = jnp.where(z == 0, pair[0], 0.0) + jnp.where(z == 8, roll(pair[1], 8), 0.0)
        for k in (1, 2, 4):
            up = up + roll(up, -k)
            down = down + roll(down, k)
        fsend[0, q] = up
        fsend[1, q] = down
        return 0

    lax.fori_loop(0, 8, pack_flags, 0)

    def flag_copy(side):
        return pltpu.make_async_remote_copy(
            src_ref=fsend.at[side],
            dst_ref=fland.at[side],
            send_sem=fsend_sem.at[side],
            recv_sem=frecv_sem.at[side],
            device_id={"dev": to[side]},
            device_id_type=MESH,
        )

    def value_copy(step, side, r):
        part = pl.ds(r * 2, 2)
        return pltpu.make_async_remote_copy(
            src_ref=(send1, send2)[step].at[side, part],
            dst_ref=(land1, land2)[step].at[side, part],
            send_sem=send_sem.at[step, side, r],
            recv_sem=recv_sem.at[step, side, r],
            device_id={"dev": to[side]},
            device_id_type=MESH,
        )

    fetch_near.wait()
    near = near_ref[...]
    near = jnp.concatenate([near, near], axis=0)
    entry = {d: jnp.broadcast_to(near[:, k : k + 1], (8, LANES)) for k, d in enumerate(VEL[1:])}
    for k, d in enumerate(VEL[1:]):
        slot, there = entry[d] & 3, entry[d] >= 0
        if d[1] == 0:
            index = slot + 4 * half
        else:
            own_half = half == (1 if d[1] == -1 else 0)
            main = (d[0], 0, d[2])
            if main == (0, 0, 0):
                slot = jnp.where(own_half, row & 3, slot)
                there = own_half | there
            else:
                slot = jnp.where(own_half, entry[main] & 3, slot)
                there = (own_half & (entry[main] >= 0)) | (jnp.logical_not(own_half) & there)
            index = slot + 4 * (1 - half)
        index_ref[k] = index
        present_ref[k] = there.astype(jnp.int32)

    def look(v, d):
        k = column(d)
        found = jnp.take_along_axis(v, index_ref[k], axis=0, mode="promise_in_bounds")
        return jnp.where(present_ref[k] > 0, found, CLOSED)

    pl.semaphore_wait(barrier, 2)
    for side in range(2):
        flag_copy(side).start()

    def collide_store(c_ref, x, k, g, packed):
        out = collide(g, rate)
        fluid = flags_ref[x] > 0
        for i in range(19):
            c_ref[i, x + 1] = jnp.where(fluid, out[i], CLOSED)
        for side, (members, source) in enumerate(((UP, 15), (DOWN, 0))):
            for p, i in enumerate(members):
                moved = roll(out[i], 8 * k + p - source)
                if packed[side] is None:
                    packed[side] = moved
                else:
                    packed[side] = jnp.where(z == 8 * k + p, moved, packed[side])

    def collide_all(step, c_ref, load):
        send = (send1, send2)[step]

        def part(r, _):
            if step == 0:
                fetch(r).wait()
            for qq in range(2):
                packed = [None, None]
                q = 2 * r + qq
                for k in range(2):
                    x = 2 * q + k
                    collide_store(c_ref, x, k, load(x, q, k), packed)
                for side in range(2):
                    send[side, q] = packed[side]
            for side in range(2):
                value_copy(step, side, r).start()
            return 0

        lax.fori_loop(0, 4, part, 0)

    def inner(c_ref, emit):
        for i in range(1, 19):
            cx, cy, cz = VEL[i]
            if cx:
                source, rim = (16, 0) if cx == 1 else (1, 17)
                c_ref[i, rim] = look(c_ref[i, source], (-cx, 0, 0))

        def settle(i, x, v):
            cx, cy, cz = VEL[i]
            v = roll(v, 16 * cy + cz)
            shut = v == CLOSED
            if cz:
                shut = shut | z_rim[cz]
            emit(i, x, jnp.where(shut, c_ref[OPP[i], x + 1], v))

        def part(r, _):
            for k in range(2):
                x = 2 * r + k
                emit(0, x, c_ref[0, x + 1])
                for i in range(1, 19):
                    cx, cy, cz = VEL[i]
                    v = c_ref[i, x + 1 - cx]
                    if cy:
                        v = jnp.where(y_rim[cy], look(v, (0, -cy, 0)), v)
                    settle(i, x, v)
            return 0

        lax.fori_loop(0, 8, part, 0)
        for i in range(1, 19):
            cx, cy, cz = VEL[i]
            if cx and cy:
                source, rim, x = (16, 0, 0) if cx == 1 else (1, 17, 15)
                v = jnp.where(y_rim[cy], look(c_ref[i, source], (-cx, -cy, 0)), c_ref[i, rim])
                settle(i, x, v)

    def arrive(step):
        land = (land1, land2)[step]
        for side in range(2):
            for r in range(4):
                value_copy(step, side, r).wait()
        for side, dz in ((0, -1), (1, 1)):
            for q in range(8):
                v = jnp.where(fland[side, q] > 0.0, land[side, q], CLOSED)
                face = look(v, (0, 0, dz))
                rim_ref[side, q + 1] = face
                for n, cy in enumerate((1, -1)):
                    rim_y_ref[side, n, q] = jnp.where(y_rim[cy], look(v, (0, -cy, dz)), face)
                if q == 7:
                    rim_ref[side, 0] = look(v, (-1, 0, dz))
                if q == 0:
                    rim_ref[side, 9] = look(v, (1, 0, dz))

    def outer(i, q, k, current):
        cx, cy, cz = VEL[i]
        side = 0 if cz == 1 else 1
        p = (UP if cz == 1 else DOWN).index(i)
        if cy:
            v, place = rim_y_ref[side, 0 if cy == 1 else 1, q], k
        else:
            v, place = rim_ref[side, q + 1 + (k - cx) // 2], (k - cx) % 2
        v = roll(v, (0 if cz == 1 else 15) - (8 * place + p) + 16 * cy)
        return jnp.where(z_rim[cz] & (v != CLOSED), v, current)

    collide_all(0, c1_ref, lambda x, q, k: [x_ref[i, x] for i in range(19)])

    def keep(i, x, v):
        g1_ref[i, x] = v

    inner(c1_ref, keep)
    for side in range(2):
        flag_copy(side).wait()
    arrive(0)

    def load_second(x, q, k):
        g = [g1_ref[i, x] for i in range(19)]
        return [outer(i, q, k, g[i]) if VEL[i][2] else g[i] for i in range(19)]

    collide_all(1, c2_ref, load_second)

    def finish(i, x, v):
        out_ref[i, x] = jnp.where(flags_ref[x] > 0, v, x_ref[i, x])

    def keep_or_finish(i, x, v):
        if VEL[i][2]:
            g1_ref[i, x] = v
        else:
            finish(i, x, v)

    inner(c2_ref, keep_or_finish)
    arrive(1)

    def last(q, _):
        for k in range(2):
            x = 2 * q + k
            for i in UP + DOWN:
                finish(i, x, outer(i, q, k, g1_ref[i, x]))
        return 0

    lax.fori_loop(0, 8, last, 0)


def body(populations, fluid_flags, neighbours, relax_rate):
    f32, i32 = jnp.float32, jnp.int32

    def vmem(*shape, kind=f32):
        return pltpu.VMEM(shape + (8, LANES), kind)

    tiles = populations.reshape(SLOTS, 19, 16, 2, LANES).transpose(1, 2, 3, 0, 4).reshape(19, 16, 8, LANES)
    flags = fluid_flags.reshape(SLOTS, 16, 2, LANES).transpose(1, 2, 0, 3).reshape(16, 8, LANES)
    done = pl.pallas_call(
        functools.partial(kernel, lax.axis_size("dev")),
        out_shape=jax.ShapeDtypeStruct((19, 16, 8, LANES), f32),
        in_specs=[
            pl.BlockSpec(memory_space=pltpu.HBM),
            pl.BlockSpec(memory_space=pltpu.HBM),
            pl.BlockSpec(memory_space=pltpu.HBM),
            pl.BlockSpec(memory_space=pltpu.SMEM),
        ],
        out_specs=pl.BlockSpec(memory_space=pltpu.VMEM),
        scratch_shapes=[
            vmem(19, 16),
            vmem(16, kind=i32),
            pltpu.VMEM((SLOTS, 18), i32),
            vmem(19, 18),
            vmem(19, 18),
            vmem(19, 16),
            vmem(18, kind=i32),
            vmem(18, kind=i32),
            vmem(2, 8),
            vmem(2, 8),
            vmem(2, 8),
            vmem(2, 8),
            vmem(2, 8),
            vmem(2, 8),
            vmem(2, 10),
            vmem(2, 2, 8),
            pltpu.SemaphoreType.DMA((4,)),
            pltpu.SemaphoreType.DMA((2,)),
            pltpu.SemaphoreType.DMA((2,)),
            pltpu.SemaphoreType.DMA((2,)),
            pltpu.SemaphoreType.DMA((2, 2, 4)),
            pltpu.SemaphoreType.DMA((2, 2, 4)),
        ],
        compiler_params=pltpu.CompilerParams(
            collective_id=0, has_side_effects=True, vmem_limit_bytes=40 * 2**20
        ),
        name="lattice_steps",
    )(tiles, flags, neighbours, relax_rate)
    back = done.reshape(19, 16, 2, SLOTS, LANES).transpose(3, 0, 1, 2, 4)
    return back.reshape(SLOTS, 19, CELLS)


def solution(mesh):
    placed = (
        P(("group", "dev"), None, None),
        P(("group", "dev"), None),
        P(("group", "dev"), None),
        P(("group", "dev")),
    )
    return jax.shard_map(
        body, mesh=mesh, in_specs=placed, out_specs=P(("group", "dev"), None, None), check_vma=False
    )
```

```python
import functools

import jax
import jax.numpy as jnp
import numpy as np
from jax import lax
from jax.experimental import pallas as pl
from jax.experimental.pallas import tpu as pltpu
from jax.sharding import PartitionSpec as P

SLOTS = 4
CELLS = 4096
LANES = 128
MESH = pl.DeviceIdType.MESH
CLOSED = np.float32(np.inf)


def velocities():
    found = [(0, 0, 0)]
    for axis in range(3):
        for sign in (1, -1):
            v = [0, 0, 0]
            v[axis] = sign
            found.append(tuple(v))
    for one, two in ((0, 1), (0, 2), (1, 2)):
        for sign_one in (1, -1):
            for sign_two in (1, -1):
                v = [0, 0, 0]
                v[one] = sign_one
                v[two] = sign_two
                found.append(tuple(v))
    return found


VEL = velocities()
OPP = [VEL.index(tuple(-c for c in v)) for v in VEL]
UP = [i for i, v in enumerate(VEL) if v[2] == 1]
DOWN = [i for i, v in enumerate(VEL) if v[2] == -1]

def column(direction):
    return VEL.index(direction) - 1


def collide(g, rate):
    sx, dx = g[1] + g[2], g[1] - g[2]
    sy, dy = g[3] + g[4], g[3] - g[4]
    sz, dz = g[5] + g[6], g[5] - g[6]

    def plane(first):
        a, b = g[first] + g[first + 3], g[first + 1] + g[first + 2]
        c, d = g[first] - g[first + 3], g[first + 1] - g[first + 2]
        return a + b, a - b, c + d, c - d

    exy, qxy, x1, y1 = plane(7)
    exz, qxz, x2, z1 = plane(11)
    eyz, qyz, y2, z2 = plane(15)
    sixth = np.float32(1 / 6)
    ux = (dx + 0.5 * (x1 + x2)) * sixth
    uy = (dy + 0.5 * (y1 + y2)) * sixth
    uz = (dz + 0.5 * (z1 + z2)) * sixth
    xx = (sx + sx) + (exy + exz)
    yy = (sy + sy) + (exy + eyz)
    zz = (sz + sz) + (exz + eyz)
    total = xx + yy + zz
    edges = exy + exz + eyz
    density = g[0] * np.float32(1 / 3) + (total - edges) * np.float32(1 / 36)
    ux2, uy2, uz2 = ux * ux, uy * uy, uz * uz
    u2 = ux2 + uy2 + uz2
    keep = 1.0 - rate
    quarter = 0.25 * keep
    base = density - u2 * sixth
    face = base + (keep * np.float32(1 / 3)) * u2 - (quarter * np.float32(1 / 3)) * total
    half_less = 0.5 - keep
    out = [None] * 19
    out[0] = base
    for first, along, u, square in ((1, xx, ux, ux2), (3, yy, uy, uy2), (5, zz, uz, uz2)):
        even = face + quarter * along + half_less * square
        out[first], out[first + 1] = even + u, even - u
    hx, hy, hz = 0.5 * ux2, 0.5 * uy2, 0.5 * uz2
    for first, ua, ub, ha, hb, q in (
        (7, ux, uy, hx, hy, qxy),
        (11, ux, uz, hx, hz, qxz),
        (15, uy, uz, hy, hz, qyz),
    ):
        cross = rate * (ua * ub) + quarter * q
        even = base + (ha + hb)
        plus, minus = even + cross, even - cross
        add, sub = ua + ub, ua - ub
        out[first], out[first + 3] = plus + add, plus - add
        out[first + 1], out[first + 2] = minus + sub, minus - sub
    return out


def roll(v, shift):
    shift = shift % LANES
    return v if shift == 0 else pltpu.roll(v, shift, 1)


def kernel(
    n_dev,
    x_hbm,
    flags_hbm,
    near_hbm,
    rate_ref,
    out_ref,
    x_ref,
    flags_ref,
    near_ref,
    c1_ref,
    c2_ref,
    g1_ref,
    index_ref,
    present_ref,
    fsend,
    fland,
    send1,
    send2,
    land1,
    land2,
    rim_ref,
    rim_y_ref,
    in_sem,
    small_sem,
    fsend_sem,
    frecv_sem,
    send_sem,
    recv_sem,
):
    me = lax.axis_index("dev")
    to = (lax.min(me + 1, n_dev - 1), lax.max(me - 1, 0))
    sends = (me < n_dev - 1, me > 0)
    hears = (me > 0, me < n_dev - 1)

    barrier = pltpu.get_barrier_semaphore()
    for side in range(2):

        @pl.when(sends[side])
        def _(side=side):
            pl.semaphore_signal(barrier, inc=1, device_id={"dev": to[side]}, device_id_type=MESH)

    def fetch(r):
        part = pl.ds(r * 4, 4)
        return pltpu.make_async_copy(x_hbm.at[:, part], x_ref.at[:, part], in_sem.at[r])

    fetch_flags = pltpu.make_async_copy(flags_hbm, flags_ref, small_sem.at[0])
    fetch_near = pltpu.make_async_copy(near_hbm, near_ref, small_sem.at[1])
    fetch_flags.start()
    fetch_near.start()
    for r in range(4):
        fetch(r).start()

    lane = lax.broadcasted_iota(jnp.int32, (8, LANES), 1)
    row = lax.broadcasted_iota(jnp.int32, (8, LANES), 0)
    z = lane & 15
    z_rim = {1: z == 0, -1: z == 15}
    y_rim = {1: lane >= 112, -1: lane < 16}
    half = row >> 2

    rate = jnp.full((8, LANES), rate_ref[0], jnp.float32)
    for s in range(1, SLOTS):
        rate = jnp.where((row & 3) == s, rate_ref[s], rate)

    fetch_flags.wait()

    for q in range(8):
        pair = [(flags_ref[2 * q + k] > 0).astype(jnp.float32) for k in range(2)]
        up = jnp.where(z == 7, roll(pair[0], -8), 0.0) + jnp.where(z == 15, pair[1], 0.0)
        down = jnp.where(z == 0, pair[0], 0.0) + jnp.where(z == 8, roll(pair[1], 8), 0.0)
        for k in (1, 2, 4):
            up = up + roll(up, -k)
            down = down + roll(down, k)
        fsend[0, q] = up
        fsend[1, q] = down

    def flag_copy(side):
        return pltpu.make_async_remote_copy(
            src_ref=fsend.at[side],
            dst_ref=fland.at[side],
            send_sem=fsend_sem.at[side],
            recv_sem=frecv_sem.at[side],
            device_id={"dev": to[side]},
            device_id_type=MESH,
        )

    def value_copy(step, side, r):
        part = pl.ds(r * 2, 2)
        return pltpu.make_async_remote_copy(
            src_ref=(send1, send2)[step].at[side, part],
            dst_ref=(land1, land2)[step].at[side, part],
            send_sem=send_sem.at[step, side, r],
            recv_sem=recv_sem.at[step, side, r],
            device_id={"dev": to[side]},
            device_id_type=MESH,
        )

    fetch_near.wait()
    near = near_ref[...]
    near = jnp.concatenate([near, near], axis=0)
    entry = {d: jnp.broadcast_to(near[:, k : k + 1], (8, LANES)) for k, d in enumerate(VEL[1:])}
    for k, d in enumerate(VEL[1:]):
        slot, there = entry[d] & 3, entry[d] >= 0
        if d[1] == 0:
            index = slot + 4 * half
        else:
            own_half = half == (1 if d[1] == -1 else 0)
            main = (d[0], 0, d[2])
            if main == (0, 0, 0):
                slot = jnp.where(own_half, row & 3, slot)
                there = own_half | there
            else:
                slot = jnp.where(own_half, entry[main] & 3, slot)
                there = (own_half & (entry[main] >= 0)) | (jnp.logical_not(own_half) & there)
            index = slot + 4 * (1 - half)
        index_ref[k] = index
        present_ref[k] = there.astype(jnp.int32)

    def look(v, d):
        k = column(d)
        found = jnp.take_along_axis(v, index_ref[k], axis=0, mode="promise_in_bounds")
        return jnp.where(present_ref[k] > 0, found, CLOSED)

    def start(copy, side):
        @pl.when(sends[side])
        def _():
            copy.start()

    def sent(copy, side):
        @pl.when(sends[side])
        def _():
            copy.wait_send()

    def landed(copy, side):
        @pl.when(hears[side])
        def _():
            copy.wait_recv()

    pl.semaphore_wait(barrier, jnp.where(hears[0] & hears[1], 2, 1))
    for side in range(2):
        start(flag_copy(side), side)

    def collide_store(c_ref, x, k, g, packed):
        out = collide(g, rate)
        fluid = flags_ref[x] > 0
        for i in range(19):
            c_ref[i, x + 1] = jnp.where(fluid, out[i], CLOSED)
        for side, (members, source) in enumerate(((UP, 15), (DOWN, 0))):
            for p, i in enumerate(members):
                moved = roll(out[i], 8 * k + p - source)
                if packed[side] is None:
                    packed[side] = moved
                else:
                    packed[side] = jnp.where(z == 8 * k + p, moved, packed[side])

    def collide_all(step, c_ref, load):
        send = (send1, send2)[step]

        def part(r, _):
            if step == 0:
                fetch(r).wait()
            for qq in range(2):
                packed = [None, None]
                q = 2 * r + qq
                for k in range(2):
                    x = 2 * q + k
                    collide_store(c_ref, x, k, load(x, q, k), packed)
                for side in range(2):
                    send[side, q] = packed[side]
            for side in range(2):
                start(value_copy(step, side, r), side)
            return 0

        lax.fori_loop(0, 4, part, 0)

    def inner(c_ref, emit):
        for i in range(1, 19):
            cx, cy, cz = VEL[i]
            if cx:
                source, rim = (16, 0) if cx == 1 else (1, 17)
                c_ref[i, rim] = look(c_ref[i, source], (-cx, 0, 0))

        def settle(i, x, v):
            cx, cy, cz = VEL[i]
            v = roll(v, 16 * cy + cz)
            shut = v == CLOSED
            if cz:
                shut = shut | z_rim[cz]
            emit(i, x, jnp.where(shut, c_ref[OPP[i], x + 1], v))

        def part(r, _):
            for k in range(2):
                x = 2 * r + k
                emit(0, x, c_ref[0, x + 1])
                for i in range(1, 19):
                    cx, cy, cz = VEL[i]
                    v = c_ref[i, x + 1 - cx]
                    if cy:
                        v = jnp.where(y_rim[cy], look(v, (0, -cy, 0)), v)
                    settle(i, x, v)
            return 0

        lax.fori_loop(0, 8, part, 0)
        for i in range(1, 19):
            cx, cy, cz = VEL[i]
            if cx and cy:
                source, rim, x = (16, 0, 0) if cx == 1 else (1, 17, 15)
                v = jnp.where(y_rim[cy], look(c_ref[i, source], (-cx, -cy, 0)), c_ref[i, rim])
                settle(i, x, v)

    def arrive(step):
        land = (land1, land2)[step]
        for side in range(2):
            for r in range(4):
                landed(value_copy(step, side, r), side)
        for side, dz in ((0, -1), (1, 1)):
            for q in range(8):
                v = jnp.where(fland[side, q] > 0.0, land[side, q], CLOSED)
                face = look(v, (0, 0, dz))
                rim_ref[side, q + 1] = face
                for n, cy in enumerate((1, -1)):
                    rim_y_ref[side, n, q] = jnp.where(y_rim[cy], look(v, (0, -cy, dz)), face)
                if q == 7:
                    rim_ref[side, 0] = look(v, (-1, 0, dz))
                if q == 0:
                    rim_ref[side, 9] = look(v, (1, 0, dz))

    def outer(i, q, k, current):
        cx, cy, cz = VEL[i]
        side = 0 if cz == 1 else 1
        p = (UP if cz == 1 else DOWN).index(i)
        if cy:
            v, place = rim_y_ref[side, 0 if cy == 1 else 1, q], k
        else:
            v, place = rim_ref[side, q + 1 + (k - cx) // 2], (k - cx) % 2
        v = roll(v, (0 if cz == 1 else 15) - (8 * place + p) + 16 * cy)
        return jnp.where(z_rim[cz] & (v != CLOSED), v, current)

    collide_all(0, c1_ref, lambda x, q, k: [x_ref[i, x] for i in range(19)])

    def keep(i, x, v):
        g1_ref[i, x] = v

    inner(c1_ref, keep)
    for side in range(2):
        landed(flag_copy(side), side)
    arrive(0)

    def load_second(x, q, k):
        g = [g1_ref[i, x] for i in range(19)]
        return [outer(i, q, k, g[i]) if VEL[i][2] else g[i] for i in range(19)]

    collide_all(1, c2_ref, load_second)

    def finish(i, x, v):
        out_ref[i, x] = jnp.where(flags_ref[x] > 0, v, x_ref[i, x])

    def keep_or_finish(i, x, v):
        if VEL[i][2]:
            g1_ref[i, x] = v
        else:
            finish(i, x, v)

    inner(c2_ref, keep_or_finish)
    arrive(1)

    def last(q, _):
        for k in range(2):
            x = 2 * q + k
            for i in UP + DOWN:
                finish(i, x, outer(i, q, k, g1_ref[i, x]))
        return 0

    lax.fori_loop(0, 8, last, 0)
    for side in range(2):
        sent(flag_copy(side), side)
        for step in range(2):
            for r in range(4):
                sent(value_copy(step, side, r), side)


def body(populations, fluid_flags, neighbours, relax_rate):
    f32, i32 = jnp.float32, jnp.int32

    def vmem(*shape, kind=f32):
        return pltpu.VMEM(shape + (8, LANES), kind)

    tiles = populations.reshape(SLOTS, 19, 16, 2, LANES).transpose(1, 2, 3, 0, 4).reshape(19, 16, 8, LANES)
    flags = fluid_flags.reshape(SLOTS, 16, 2, LANES).transpose(1, 2, 0, 3).reshape(16, 8, LANES)
    done = pl.pallas_call(
        functools.partial(kernel, lax.axis_size("dev")),
        out_shape=jax.ShapeDtypeStruct((19, 16, 8, LANES), f32),
        in_specs=[
            pl.BlockSpec(memory_space=pltpu.HBM),
            pl.BlockSpec(memory_space=pltpu.HBM),
            pl.BlockSpec(memory_space=pltpu.HBM),
            pl.BlockSpec(memory_space=pltpu.SMEM),
        ],
        out_specs=pl.BlockSpec(memory_space=pltpu.VMEM),
        scratch_shapes=[
            vmem(19, 16),
            vmem(16, kind=i32),
            pltpu.VMEM((SLOTS, 18), i32),
            vmem(19, 18),
            vmem(19, 18),
            vmem(19, 16),
            vmem(18, kind=i32),
            vmem(18, kind=i32),
            vmem(2, 8),
            vmem(2, 8),
            vmem(2, 8),
            vmem(2, 8),
            vmem(2, 8),
            vmem(2, 8),
            vmem(2, 10),
            vmem(2, 2, 8),
            pltpu.SemaphoreType.DMA((4,)),
            pltpu.SemaphoreType.DMA((2,)),
            pltpu.SemaphoreType.DMA((2,)),
            pltpu.SemaphoreType.DMA((2,)),
            pltpu.SemaphoreType.DMA((2, 2, 4)),
            pltpu.SemaphoreType.DMA((2, 2, 4)),
        ],
        compiler_params=pltpu.CompilerParams(
            collective_id=0, has_side_effects=True, vmem_limit_bytes=62 * 2**20
        ),
        name="lattice_steps",
    )(tiles, flags, neighbours, relax_rate)
    back = done.reshape(19, 16, 2, SLOTS, LANES).transpose(3, 0, 1, 2, 4)
    return back.reshape(SLOTS, 19, CELLS)


def solution(mesh):
    placed = (
        P(("group", "dev"), None, None),
        P(("group", "dev"), None),
        P(("group", "dev"), None),
        P(("group", "dev")),
    )
    return jax.shard_map(
        body, mesh=mesh, in_specs=placed, out_specs=P(("group", "dev"), None, None), check_vma=False
    )
```

```python
import functools

import jax
import jax.numpy as jnp
import numpy as np
from jax import lax
from jax.experimental import pallas as pl
from jax.experimental.pallas import tpu as pltpu
from jax.sharding import PartitionSpec as P

SLOTS = 4
CELLS = 4096
LANES = 128
INNER = 4
MESH = pl.DeviceIdType.MESH
CLOSED = np.float32(np.inf)


def velocities():
    found = [(0, 0, 0)]
    for axis in range(3):
        for sign in (1, -1):
            v = [0, 0, 0]
            v[axis] = sign
            found.append(tuple(v))
    for one, two in ((0, 1), (0, 2), (1, 2)):
        for sign_one in (1, -1):
            for sign_two in (1, -1):
                v = [0, 0, 0]
                v[one] = sign_one
                v[two] = sign_two
                found.append(tuple(v))
    return found


VEL = velocities()
OPP = [VEL.index(tuple(-c for c in v)) for v in VEL]
UP = [i for i, v in enumerate(VEL) if v[2] == 1]
DOWN = [i for i, v in enumerate(VEL) if v[2] == -1]

def column(direction):
    return VEL.index(direction) - 1


def collide(g, rate):
    sx, dx = g[1] + g[2], g[1] - g[2]
    sy, dy = g[3] + g[4], g[3] - g[4]
    sz, dz = g[5] + g[6], g[5] - g[6]

    def plane(first):
        a, b = g[first] + g[first + 3], g[first + 1] + g[first + 2]
        c, d = g[first] - g[first + 3], g[first + 1] - g[first + 2]
        return a + b, a - b, c + d, c - d

    exy, qxy, x1, y1 = plane(7)
    exz, qxz, x2, z1 = plane(11)
    eyz, qyz, y2, z2 = plane(15)
    sixth = np.float32(1 / 6)
    ux = (dx + 0.5 * (x1 + x2)) * sixth
    uy = (dy + 0.5 * (y1 + y2)) * sixth
    uz = (dz + 0.5 * (z1 + z2)) * sixth
    xx = (sx + sx) + (exy + exz)
    yy = (sy + sy) + (exy + eyz)
    zz = (sz + sz) + (exz + eyz)
    total = xx + yy + zz
    edges = exy + exz + eyz
    density = g[0] * np.float32(1 / 3) + (total - edges) * np.float32(1 / 36)
    ux2, uy2, uz2 = ux * ux, uy * uy, uz * uz
    u2 = ux2 + uy2 + uz2
    keep = 1.0 - rate
    quarter = 0.25 * keep
    base = density - u2 * sixth
    face = base + (keep * np.float32(1 / 3)) * u2 - (quarter * np.float32(1 / 3)) * total
    half_less = 0.5 - keep
    out = [None] * 19
    out[0] = base
    for first, along, u, square in ((1, xx, ux, ux2), (3, yy, uy, uy2), (5, zz, uz, uz2)):
        even = face + quarter * along + half_less * square
        out[first], out[first + 1] = even + u, even - u
    hx, hy, hz = 0.5 * ux2, 0.5 * uy2, 0.5 * uz2
    for first, ua, ub, ha, hb, q in (
        (7, ux, uy, hx, hy, qxy),
        (11, ux, uz, hx, hz, qxz),
        (15, uy, uz, hy, hz, qyz),
    ):
        cross = rate * (ua * ub) + quarter * q
        even = base + (ha + hb)
        plus, minus = even + cross, even - cross
        add, sub = ua + ub, ua - ub
        out[first], out[first + 3] = plus + add, plus - add
        out[first + 1], out[first + 2] = minus + sub, minus - sub
    return out


def roll(v, shift):
    shift = shift % LANES
    return v if shift == 0 else pltpu.roll(v, shift, 1)


def turn(v, shift):
    return roll(v, shift) if isinstance(shift, int) else pltpu.roll(v, shift & (LANES - 1), 1)


def kernel(
    n_dev,
    x_hbm,
    flags_hbm,
    near_hbm,
    rate_ref,
    out_ref,
    x_ref,
    flags_ref,
    near_ref,
    c1_ref,
    c2_ref,
    g1_ref,
    index_ref,
    absent_ref,
    layer_ref,
    halo_ref,
    fsend,
    fland,
    send1,
    send2,
    land1,
    land2,
    in_sem,
    small_sem,
    fsend_sem,
    frecv_sem,
    send_sem,
    recv_sem,
):
    me = lax.axis_index("dev")
    to = (lax.min(me + 1, n_dev - 1), lax.max(me - 1, 0))
    sends = (me < n_dev - 1, me > 0)
    hears = (me > 0, me < n_dev - 1)

    def fetch(r):
        part = pl.ds(r * 4, 4)
        return pltpu.make_async_copy(x_hbm.at[:, part], x_ref.at[:, part], in_sem.at[r])

    fetch_flags = pltpu.make_async_copy(flags_hbm, flags_ref, small_sem.at[0])
    fetch_near = pltpu.make_async_copy(near_hbm, near_ref, small_sem.at[1])
    fetch_flags.start()
    fetch_near.start()
    for r in range(4):
        fetch(r).start()

    barrier = pltpu.get_barrier_semaphore()
    for side in range(2):

        @pl.when(sends[side])
        def _(side=side):
            pl.semaphore_signal(barrier, inc=1, device_id={"dev": to[side]}, device_id_type=MESH)

    lane = lax.broadcasted_iota(jnp.int32, (8, LANES), 1)
    row = lax.broadcasted_iota(jnp.int32, (8, LANES), 0)
    z = lane & 15
    z_rim = {1: z == 0, -1: z == 15}
    y_rim = {1: lane >= 112, -1: lane < 16}
    half = row >> 2

    rate = jnp.full((8, LANES), rate_ref[0], jnp.float32)
    for s in range(1, SLOTS):
        rate = jnp.where((row & 3) == s, rate_ref[s], rate)

    fetch_near.wait()
    near = near_ref[...]
    near = jnp.concatenate([near, near], axis=0)
    entry = {d: jnp.broadcast_to(near[:, k : k + 1], (8, LANES)) for k, d in enumerate(VEL[1:])}
    for k, d in enumerate(VEL[1:]):
        slot, there = entry[d] & 3, entry[d] >= 0
        if d[1] == 0:
            index = slot + 4 * half
        else:
            own_half = half == (1 if d[1] == -1 else 0)
            main = (d[0], 0, d[2])
            if main == (0, 0, 0):
                slot = jnp.where(own_half, row & 3, slot)
                there = own_half | there
            else:
                slot = jnp.where(own_half, entry[main] & 3, slot)
                there = (own_half & (entry[main] >= 0)) | (jnp.logical_not(own_half) & there)
            index = slot + 4 * (1 - half)
        index_ref[k] = index
        absent_ref[k] = jnp.where(there, 0.0, CLOSED)

    def look(v, d):
        k = column(d)
        return jnp.take_along_axis(v, index_ref[k], axis=0, mode="promise_in_bounds") + absent_ref[k]

    def gathered(x, v, layer, into):
        moved = turn(v, x - layer)
        return moved if into is None else jnp.where(z == x, moved, into)

    fetch_flags.wait()
    wet = [None, None]
    for x in range(16):
        flag = (flags_ref[x] > 0).astype(jnp.float32)
        for side, layer in enumerate((15, 0)):
            wet[side] = gathered(x, flag, layer, wet[side])
    for side in range(2):
        fsend[side] = wet[side]

    def flag_copy(side):
        return pltpu.make_async_remote_copy(
            src_ref=fsend.at[side],
            dst_ref=fland.at[side],
            send_sem=fsend_sem.at[side],
            recv_sem=frecv_sem.at[side],
            device_id={"dev": to[side]},
            device_id_type=MESH,
        )

    def value_copy(step, side):
        return pltpu.make_async_remote_copy(
            src_ref=(send1, send2)[step].at[side],
            dst_ref=(land1, land2)[step].at[side],
            send_sem=send_sem.at[step, side],
            recv_sem=recv_sem.at[step, side],
            device_id={"dev": to[side]},
            device_id_type=MESH,
        )

    def first(r, packed):
        fetch(r).wait()
        packed = list(packed)
        for k in range(4):
            x = 4 * r + k
            out = collide([x_ref[i, x] for i in range(19)], rate)
            fluid = flags_ref[x] > 0
            for i in range(19):
                c1_ref[i, x + 1] = jnp.where(fluid, out[i], CLOSED)
            for n, i in enumerate(UP + DOWN):
                packed[n] = gathered(x, out[i], 15 if n < 5 else 0, packed[n])
        return tuple(packed)

    packed = lax.fori_loop(0, 4, first, (jnp.zeros((8, LANES), jnp.float32),) * 10)
    for n in range(10):
        send1[n // 5, n % 5] = packed[n]

    pl.semaphore_wait(barrier, jnp.where(hears[0] & hears[1], 2, 1))
    for side in range(2):

        @pl.when(sends[side])
        def _(side=side):
            value_copy(0, side).start()
            flag_copy(side).start()

    def inner(c_ref, emit):
        for i in range(1, 19):
            cx, cy, cz = VEL[i]
            if cx:
                source, rim = (16, 0) if cx == 1 else (1, 17)
                c_ref[i, rim] = look(c_ref[i, source], (-cx, 0, 0))

        def settle(i, x, v):
            cx, cy, cz = VEL[i]
            v = roll(v, 16 * cy + cz)
            shut = v == CLOSED
            if cz:
                shut = shut | z_rim[cz]
            emit(i, x, jnp.where(shut, c_ref[OPP[i], x + 1], v))

        def part(r, _):
            for k in range(INNER):
                x = INNER * r + k
                emit(0, x, c_ref[0, x + 1])
                for i in range(1, 19):
                    cx, cy, cz = VEL[i]
                    v = c_ref[i, x + 1 - cx]
                    if cy:
                        v = jnp.where(y_rim[cy], look(v, (0, -cy, 0)), v)
                    settle(i, x, v)
            return 0

        lax.fori_loop(0, 16 // INNER, part, 0)
        for i in range(1, 19):
            cx, cy, cz = VEL[i]
            if cx and cy:
                source, rim, x = (16, 0, 0) if cx == 1 else (1, 17, 15)
                v = jnp.where(y_rim[cy], look(c_ref[i, source], (-cx, -cy, 0)), c_ref[i, rim])
                settle(i, x, v)

    def arrive(step, side):
        land = (land1, land2)[step]

        @pl.when(hears[side])
        def _():
            if step == 0:
                flag_copy(side).wait_recv()
            value_copy(step, side).wait_recv()

        halo = []
        for p, i in enumerate((UP, DOWN)[side]):
            cx, cy, cz = VEL[i]
            v = jnp.where(fland[side] > 0.0, land[side, p], CLOSED)
            face = look(v, (0, 0, -cz))
            if cx:
                away = roll(look(v, (-cx, 0, -cz)), -15 * cx)
                v = jnp.where(z == (0 if cx == 1 else 15), away, roll(face, cx))
            elif cy:
                v = roll(jnp.where(y_rim[cy], look(v, (0, -cy, -cz)), face), 16 * cy)
            else:
                v = face
            halo.append(v)
            halo_ref[step, side, p] = v
        return halo

    def outer(step, i, x, current):
        cz = VEL[i][2]
        side = 0 if cz == 1 else 1
        v = turn(halo_ref[step, side, (UP, DOWN)[side].index(i)], (0 if cz == 1 else 15) - x)
        return jnp.where(z_rim[cz] & (v != CLOSED), v, current)

    def keep(i, x, v):
        g1_ref[i, x] = v

    inner(c1_ref, keep)

    def gather_layers(i, _):
        low, high = None, None
        for x in range(16):
            v = g1_ref[i, x]
            low, high = gathered(x, v, 0, low), gathered(x, v, 15, high)
        layer_ref[0, i] = low
        layer_ref[1, i] = high
        return 0

    lax.fori_loop(0, 19, gather_layers, 0)

    for side in range(2):
        halo = arrive(0, side)
        g = [layer_ref[side, i] for i in range(19)]
        for i, v in zip((UP, DOWN)[side], halo):
            g[i] = jnp.where(v != CLOSED, v, g[i])
        out = collide(g, rate)
        for p, i in enumerate((DOWN, UP)[side]):
            send2[1 - side, p] = out[i]

        @pl.when(sends[1 - side])
        def _(side=side):
            value_copy(1, 1 - side).start()

    def second(r, _):
        for k in range(4):
            x = 4 * r + k
            g = [g1_ref[i, x] for i in range(19)]
            out = collide([outer(0, i, x, g[i]) if VEL[i][2] else g[i] for i in range(19)], rate)
            fluid = flags_ref[x] > 0
            for i in range(19):
                c2_ref[i, x + 1] = jnp.where(fluid, out[i], CLOSED)
        return 0

    lax.fori_loop(0, 4, second, 0)

    def finish(i, x, v):
        out_ref[i, x] = jnp.where(flags_ref[x] > 0, v, x_ref[i, x])

    def keep_or_finish(i, x, v):
        if VEL[i][2]:
            g1_ref[i, x] = v
        else:
            finish(i, x, v)

    inner(c2_ref, keep_or_finish)
    for side in range(2):
        arrive(1, side)

    def last(r, _):
        for k in range(4):
            x = 4 * r + k
            for i in UP + DOWN:
                finish(i, x, outer(1, i, x, g1_ref[i, x]))
        return 0

    lax.fori_loop(0, 4, last, 0)
    for side in range(2):

        @pl.when(sends[side])
        def _(side=side):
            flag_copy(side).wait_send()
            value_copy(0, side).wait_send()
            value_copy(1, side).wait_send()


def body(populations, fluid_flags, neighbours, relax_rate):
    f32, i32 = jnp.float32, jnp.int32

    def vmem(*shape, kind=f32):
        return pltpu.VMEM(shape + (8, LANES), kind)

    tiles = populations.reshape(SLOTS, 19, 16, 2, LANES).transpose(1, 2, 3, 0, 4).reshape(19, 16, 8, LANES)
    flags = fluid_flags.reshape(SLOTS, 16, 2, LANES).transpose(1, 2, 0, 3).reshape(16, 8, LANES)
    done = pl.pallas_call(
        functools.partial(kernel, lax.axis_size("dev")),
        out_shape=pltpu.VMEM((19, 16, 8, LANES), f32),
        in_specs=[
            pl.BlockSpec(memory_space=pltpu.HBM),
            pl.BlockSpec(memory_space=pltpu.HBM),
            pl.BlockSpec(memory_space=pltpu.HBM),
            pl.BlockSpec(memory_space=pltpu.SMEM),
        ],
        out_specs=pl.BlockSpec(memory_space=pltpu.VMEM),
        scratch_shapes=[
            vmem(19, 16),
            vmem(16, kind=i32),
            pltpu.VMEM((SLOTS, 18), i32),
            vmem(19, 18),
            vmem(19, 18),
            vmem(19, 16),
            vmem(18, kind=i32),
            vmem(18),
            vmem(2, 19),
            vmem(2, 2, 5),
            vmem(2),
            vmem(2),
            vmem(2, 5),
            vmem(2, 5),
            vmem(2, 5),
            vmem(2, 5),
            pltpu.SemaphoreType.DMA((4,)),
            pltpu.SemaphoreType.DMA((2,)),
            pltpu.SemaphoreType.DMA((2,)),
            pltpu.SemaphoreType.DMA((2,)),
            pltpu.SemaphoreType.DMA((2, 2)),
            pltpu.SemaphoreType.DMA((2, 2)),
        ],
        compiler_params=pltpu.CompilerParams(
            collective_id=0, has_side_effects=True, vmem_limit_bytes=62 * 2**20
        ),
        name="lattice_steps",
    )(tiles, flags, neighbours, relax_rate)
    back = done.reshape(19, 16, 2, SLOTS, LANES).transpose(3, 0, 1, 2, 4)
    return back.reshape(SLOTS, 19, CELLS)


def solution(mesh):
    placed = (
        P(("group", "dev"), None, None),
        P(("group", "dev"), None),
        P(("group", "dev"), None),
        P(("group", "dev")),
    )
    return jax.shard_map(
        body, mesh=mesh, in_specs=placed, out_specs=P(("group", "dev"), None, None), check_vma=False
    )
```

```python
import functools

import jax
import jax.numpy as jnp
import numpy as np
from jax import lax
from jax.experimental import pallas as pl
from jax.experimental.pallas import tpu as pltpu
from jax.sharding import PartitionSpec as P

SLOTS = 4
CELLS = 4096
LANES = 128
INNER = 4
MESH = pl.DeviceIdType.MESH
CLOSED = np.float32(np.inf)


def velocities():
    found = [(0, 0, 0)]
    for axis in range(3):
        for sign in (1, -1):
            v = [0, 0, 0]
            v[axis] = sign
            found.append(tuple(v))
    for one, two in ((0, 1), (0, 2), (1, 2)):
        for sign_one in (1, -1):
            for sign_two in (1, -1):
                v = [0, 0, 0]
                v[one] = sign_one
                v[two] = sign_two
                found.append(tuple(v))
    return found


VEL = velocities()
OPP = [VEL.index(tuple(-c for c in v)) for v in VEL]
UP = [i for i, v in enumerate(VEL) if v[2] == 1]
DOWN = [i for i, v in enumerate(VEL) if v[2] == -1]

PLANE = [i for i, v in enumerate(VEL) if v[2] == 0]


def column(direction):
    return VEL.index(direction) - 1


def collide(g, rate):
    sx, dx = g[1] + g[2], g[1] - g[2]
    sy, dy = g[3] + g[4], g[3] - g[4]
    sz, dz = g[5] + g[6], g[5] - g[6]

    def plane(first):
        a, b = g[first] + g[first + 3], g[first + 1] + g[first + 2]
        c, d = g[first] - g[first + 3], g[first + 1] - g[first + 2]
        return a + b, a - b, c + d, c - d

    exy, qxy, x1, y1 = plane(7)
    exz, qxz, x2, z1 = plane(11)
    eyz, qyz, y2, z2 = plane(15)
    sixth = np.float32(1 / 6)
    ux = (dx + 0.5 * (x1 + x2)) * sixth
    uy = (dy + 0.5 * (y1 + y2)) * sixth
    uz = (dz + 0.5 * (z1 + z2)) * sixth
    xx = (sx + sx) + (exy + exz)
    yy = (sy + sy) + (exy + eyz)
    zz = (sz + sz) + (exz + eyz)
    total = xx + yy + zz
    edges = exy + exz + eyz
    density = g[0] * np.float32(1 / 3) + (total - edges) * np.float32(1 / 36)
    ux2, uy2, uz2 = ux * ux, uy * uy, uz * uz
    u2 = ux2 + uy2 + uz2
    keep = 1.0 - rate
    quarter = 0.25 * keep
    base = density - u2 * sixth
    face = base + (keep * np.float32(1 / 3)) * u2 - (quarter * np.float32(1 / 3)) * total
    half_less = 0.5 - keep
    out = [None] * 19
    out[0] = base
    for first, along, u, square in ((1, xx, ux, ux2), (3, yy, uy, uy2), (5, zz, uz, uz2)):
        even = face + quarter * along + half_less * square
        out[first], out[first + 1] = even + u, even - u
    hx, hy, hz = 0.5 * ux2, 0.5 * uy2, 0.5 * uz2
    for first, ua, ub, ha, hb, q in (
        (7, ux, uy, hx, hy, qxy),
        (11, ux, uz, hx, hz, qxz),
        (15, uy, uz, hy, hz, qyz),
    ):
        cross = rate * (ua * ub) + quarter * q
        even = base + (ha + hb)
        plus, minus = even + cross, even - cross
        add, sub = ua + ub, ua - ub
        out[first], out[first + 3] = plus + add, plus - add
        out[first + 1], out[first + 2] = minus + sub, minus - sub
    return out


def roll(v, shift):
    shift = shift % LANES
    return v if shift == 0 else pltpu.roll(v, shift, 1)


def turn(v, shift):
    return roll(v, shift) if isinstance(shift, int) else pltpu.roll(v, shift & (LANES - 1), 1)


def kernel(
    n_dev,
    x_hbm,
    flags_hbm,
    near_hbm,
    rate_ref,
    out_ref,
    x_ref,
    flags_ref,
    near_ref,
    c1_ref,
    c2_ref,
    g1_ref,
    index_ref,
    absent_ref,
    halo_ref,
    send1,
    send2,
    land1,
    land2,
    in_sem,
    small_sem,
    send_sem,
    recv_sem,
):
    me = lax.axis_index("dev")
    to = (lax.min(me + 1, n_dev - 1), lax.max(me - 1, 0))
    sends = (me < n_dev - 1, me > 0)
    hears = (me > 0, me < n_dev - 1)

    def fetch(r):
        part = pl.ds(r * 4, 4)
        return pltpu.make_async_copy(x_hbm.at[:, part], x_ref.at[:, part], in_sem.at[r])

    fetch_flags = pltpu.make_async_copy(flags_hbm, flags_ref, small_sem.at[0])
    fetch_near = pltpu.make_async_copy(near_hbm, near_ref, small_sem.at[1])
    fetch_flags.start()
    fetch_near.start()
    for r in range(4):
        fetch(r).start()

    barrier = pltpu.get_barrier_semaphore()
    for side in range(2):

        @pl.when(sends[side])
        def _(side=side):
            pl.semaphore_signal(barrier, inc=1, device_id={"dev": to[side]}, device_id_type=MESH)

    lane = lax.broadcasted_iota(jnp.int32, (8, LANES), 1)
    row = lax.broadcasted_iota(jnp.int32, (8, LANES), 0)
    z = lane & 15
    z_rim = {1: z == 0, -1: z == 15}
    y_rim = {1: lane >= 112, -1: lane < 16}
    half = row >> 2

    rate = jnp.full((8, LANES), rate_ref[0], jnp.float32)
    for s in range(1, SLOTS):
        rate = jnp.where((row & 3) == s, rate_ref[s], rate)

    fetch_near.wait()
    near = near_ref[...]
    near = jnp.concatenate([near, near], axis=0)
    entry = {d: jnp.broadcast_to(near[:, k : k + 1], (8, LANES)) for k, d in enumerate(VEL[1:])}
    own = {d: (e & 3, e >= 0) for d, e in entry.items()}
    theirs = {}
    for d in VEL[1:]:
        if d[2]:
            e = entry[tuple(-c for c in d)]
            slot, there = row & 3, None
            for m in range(4):
                named = pltpu.roll(e, m, 0) if m else e
                match = named == (1 - d[2]) * 4 + (row & 3)
                slot = jnp.where(match, (row - m) & 3, slot)
                there = match if there is None else there | match
            theirs[d] = (slot, there)

    for table, first_row in ((own, 0), (theirs, 18)):
        for d, (slot, there) in table.items():
            if d[1] == 0:
                index = slot + 4 * half
            else:
                own_half = half == (1 if d[1] == -1 else 0)
                main = (d[0], 0, d[2])
                main_slot, main_there = (row & 3, row >= 0) if main == (0, 0, 0) else table[main]
                slot = jnp.where(own_half, main_slot, slot)
                there = (own_half & main_there) | (jnp.logical_not(own_half) & there)
                index = slot + 4 * (1 - half)
            index_ref[first_row + column(d)] = index
            absent_ref[first_row + column(d)] = jnp.where(there, 0.0, CLOSED)

    def look(v, d):
        k = column(d)
        return jnp.take_along_axis(v, index_ref[k], axis=0, mode="promise_in_bounds") + absent_ref[k]

    def look_across(v, d, first_row=0):
        k = first_row + column(d)
        found = jnp.take_along_axis(v, index_ref[k], axis=0, mode="promise_in_bounds")
        return jnp.where(absent_ref[k] > 0.0, CLOSED, found)

    def gathered(x, v, layer, into):
        moved = turn(v, x - layer)
        return moved if into is None else jnp.where(z == x, moved, into)

    fetch_flags.wait()
    wet = [None, None]
    for x in range(16):
        flag = (flags_ref[x] > 0).astype(jnp.float32)
        for side, layer in enumerate((15, 0)):
            wet[side] = gathered(x, flag, layer, wet[side])
    for side in range(2):
        send1[side, 5] = wet[side]
        send2[side, 14] = rate

    def value_copy(step, side):
        return pltpu.make_async_remote_copy(
            src_ref=(send1, send2)[step].at[side],
            dst_ref=(land1, land2)[step].at[side],
            send_sem=send_sem.at[step, side],
            recv_sem=recv_sem.at[step, side],
            device_id={"dev": to[side]},
            device_id_type=MESH,
        )

    def first(r, packed):
        fetch(r).wait()
        packed = list(packed)
        for k in range(4):
            x = 4 * r + k
            out = collide([x_ref[i, x] for i in range(19)], rate)
            fluid = flags_ref[x] > 0
            for i in range(19):
                c1_ref[i, x + 1] = jnp.where(fluid, out[i], CLOSED)
            for n, i in enumerate(UP + DOWN):
                packed[n] = gathered(x, out[i], 15 if n < 5 else 0, packed[n])
        return tuple(packed)

    packed = lax.fori_loop(0, 4, first, (jnp.zeros((8, LANES), jnp.float32),) * 10)
    for n in range(10):
        send1[n // 5, n % 5] = packed[n]

    pl.semaphore_wait(barrier, jnp.where(hears[0] & hears[1], 2, 1))
    for side in range(2):

        @pl.when(sends[side])
        def _(side=side):
            value_copy(0, side).start()

    def inner(c_ref, emit):
        for i in range(1, 19):
            cx, cy, cz = VEL[i]
            if cx:
                source, rim = (16, 0) if cx == 1 else (1, 17)
                c_ref[i, rim] = look(c_ref[i, source], (-cx, 0, 0))

        def settle(i, x, v):
            cx, cy, cz = VEL[i]
            v = roll(v, 16 * cy + cz)
            shut = v == CLOSED
            if cz:
                shut = shut | z_rim[cz]
            emit(i, x, jnp.where(shut, c_ref[OPP[i], x + 1], v))

        def part(r, _):
            for k in range(INNER):
                x = INNER * r + k
                emit(0, x, c_ref[0, x + 1])
                for i in range(1, 19):
                    cx, cy, cz = VEL[i]
                    v = c_ref[i, x + 1 - cx]
                    if cy:
                        v = jnp.where(y_rim[cy], look(v, (0, -cy, 0)), v)
                    settle(i, x, v)
            return 0

        lax.fori_loop(0, 16 // INNER, part, 0)
        for i in range(1, 19):
            cx, cy, cz = VEL[i]
            if cx and cy:
                source, rim, x = (16, 0, 0) if cx == 1 else (1, 17, 15)
                v = jnp.where(y_rim[cy], look(c_ref[i, source], (-cx, -cy, 0)), c_ref[i, rim])
                settle(i, x, v)

    def landed(step, side):
        @pl.when(hears[side])
        def _():
            value_copy(step, side).wait_recv()

    def crossed(v, i, first_row=0):
        cx, cy, cz = VEL[i]
        face = look_across(v, (0, 0, -cz), first_row)
        if cx:
            away = roll(look_across(v, (-cx, 0, -cz), first_row), -15 * cx)
            return jnp.where(z == (0 if cx == 1 else 15), away, roll(face, cx))
        if cy:
            return roll(jnp.where(y_rim[cy], look_across(v, (0, -cy, -cz), first_row), face), 16 * cy)
        return face

    def outer(step, i, x, current):
        cz = VEL[i][2]
        side = 0 if cz == 1 else 1
        v = turn(halo_ref[step, side, (UP, DOWN)[side].index(i)], (0 if cz == 1 else 15) - x)
        return jnp.where(z_rim[cz] & (v != CLOSED), v, current)

    def keep(i, x, v):
        g1_ref[i, x] = v

    inner(c1_ref, keep)

    for side, layer in enumerate((15, 0)):
        for n, i in enumerate(PLANE + (UP, DOWN)[side]):
            into = None
            for x in range(16):
                into = gathered(x, g1_ref[i, x], layer, into)
            send2[side, n] = into

        @pl.when(sends[side])
        def _(side=side):
            value_copy(1, side).start()

    for side in range(2):
        landed(0, side)
        for p, i in enumerate((UP, DOWN)[side]):
            v = jnp.where(land1[side, 5] > 0.0, land1[side, p], CLOSED)
            halo_ref[0, side, p] = crossed(v, i)

    def second(r, _):
        for k in range(4):
            x = 4 * r + k
            g = [g1_ref[i, x] for i in range(19)]
            out = collide([outer(0, i, x, g[i]) if VEL[i][2] else g[i] for i in range(19)], rate)
            fluid = flags_ref[x] > 0
            for i in range(19):
                c2_ref[i, x + 1] = jnp.where(fluid, out[i], CLOSED)
        return 0

    lax.fori_loop(0, 4, second, 0)

    def finish(i, x, v):
        out_ref[i, x] = jnp.where(flags_ref[x] > 0, v, x_ref[i, x])

    def keep_or_finish(i, x, v):
        if VEL[i][2]:
            g1_ref[i, x] = v
        else:
            finish(i, x, v)

    inner(c2_ref, keep_or_finish)
    for side in range(2):
        theirs_out, theirs_in = (UP, DOWN) if side == 0 else (DOWN, UP)
        landed(1, side)
        g = [None] * 19
        for n, i in enumerate(PLANE + theirs_out):
            g[i] = land2[side, n]
        for p, i in enumerate(theirs_in):
            v = jnp.where(send1[1 - side, 5] > 0.0, send1[1 - side, p], CLOSED)
            v = crossed(v, i, 18)
            g[i] = jnp.where(v != CLOSED, v, land1[side, theirs_out.index(OPP[i])])
        out = collide(g, land2[side, 14])
        for p, i in enumerate(theirs_out):
            halo_ref[1, side, p] = crossed(jnp.where(land1[side, 5] > 0.0, out[i], CLOSED), i)

    def last(r, _):
        for k in range(4):
            x = 4 * r + k
            for i in UP + DOWN:
                finish(i, x, outer(1, i, x, g1_ref[i, x]))
        return 0

    lax.fori_loop(0, 4, last, 0)
    for side in range(2):

        @pl.when(sends[side])
        def _(side=side):
            value_copy(0, side).wait_send()
            value_copy(1, side).wait_send()


def body(populations, fluid_flags, neighbours, relax_rate):
    f32, i32 = jnp.float32, jnp.int32

    def vmem(*shape, kind=f32):
        return pltpu.VMEM(shape + (8, LANES), kind)

    tiles = populations.reshape(SLOTS, 19, 16, 2, LANES).transpose(1, 2, 3, 0, 4).reshape(19, 16, 8, LANES)
    flags = fluid_flags.reshape(SLOTS, 16, 2, LANES).transpose(1, 2, 0, 3).reshape(16, 8, LANES)
    done = pl.pallas_call(
        functools.partial(kernel, lax.axis_size("dev")),
        out_shape=pltpu.VMEM((19, 16, 8, LANES), f32),
        in_specs=[
            pl.BlockSpec(memory_space=pltpu.HBM),
            pl.BlockSpec(memory_space=pltpu.HBM),
            pl.BlockSpec(memory_space=pltpu.HBM),
            pl.BlockSpec(memory_space=pltpu.SMEM),
        ],
        out_specs=pl.BlockSpec(memory_space=pltpu.VMEM),
        scratch_shapes=[
            vmem(19, 16),
            vmem(16, kind=i32),
            pltpu.VMEM((SLOTS, 18), i32),
            vmem(19, 18),
            vmem(19, 18),
            vmem(19, 16),
            vmem(36, kind=i32),
            vmem(36),
            vmem(2, 2, 5),
            vmem(2, 6),
            vmem(2, 15),
            vmem(2, 6),
            vmem(2, 15),
            pltpu.SemaphoreType.DMA((4,)),
            pltpu.SemaphoreType.DMA((2,)),
            pltpu.SemaphoreType.DMA((2, 2)),
            pltpu.SemaphoreType.DMA((2, 2)),
        ],
        compiler_params=pltpu.CompilerParams(
            collective_id=0, has_side_effects=True, vmem_limit_bytes=62 * 2**20
        ),
        name="lattice_steps",
    )(tiles, flags, neighbours, relax_rate)
    back = done.reshape(19, 16, 2, SLOTS, LANES).transpose(3, 0, 1, 2, 4)
    return back.reshape(SLOTS, 19, CELLS)


def solution(mesh):
    placed = (
        P(("group", "dev"), None, None),
        P(("group", "dev"), None),
        P(("group", "dev"), None),
        P(("group", "dev")),
    )
    return jax.shard_map(
        body, mesh=mesh, in_specs=placed, out_specs=P(("group", "dev"), None, None), check_vma=False
    )
```

```python
import functools

import jax
import jax.numpy as jnp
import numpy as np
from jax import lax
from jax.experimental import pallas as pl
from jax.experimental.pallas import tpu as pltpu
from jax.sharding import PartitionSpec as P

SLOTS = 4
CELLS = 4096
LANES = 128
INNER = 4
MESH = pl.DeviceIdType.MESH
CLOSED = np.float32(np.inf)


def velocities():
    found = [(0, 0, 0)]
    for axis in range(3):
        for sign in (1, -1):
            v = [0, 0, 0]
            v[axis] = sign
            found.append(tuple(v))
    for one, two in ((0, 1), (0, 2), (1, 2)):
        for sign_one in (1, -1):
            for sign_two in (1, -1):
                v = [0, 0, 0]
                v[one] = sign_one
                v[two] = sign_two
                found.append(tuple(v))
    return found


VEL = velocities()
OPP = [VEL.index(tuple(-c for c in v)) for v in VEL]
UP = [i for i, v in enumerate(VEL) if v[2] == 1]
DOWN = [i for i, v in enumerate(VEL) if v[2] == -1]

PLANE = [i for i, v in enumerate(VEL) if v[2] == 0]


def column(direction):
    return VEL.index(direction) - 1


def collide(g, rate):
    sx, dx = g[1] + g[2], g[1] - g[2]
    sy, dy = g[3] + g[4], g[3] - g[4]
    sz, dz = g[5] + g[6], g[5] - g[6]

    def plane(first):
        a, b = g[first] + g[first + 3], g[first + 1] + g[first + 2]
        c, d = g[first] - g[first + 3], g[first + 1] - g[first + 2]
        return a + b, a - b, c + d, c - d

    exy, qxy, x1, y1 = plane(7)
    exz, qxz, x2, z1 = plane(11)
    eyz, qyz, y2, z2 = plane(15)
    sixth = np.float32(1 / 6)
    ux = (dx + 0.5 * (x1 + x2)) * sixth
    uy = (dy + 0.5 * (y1 + y2)) * sixth
    uz = (dz + 0.5 * (z1 + z2)) * sixth
    xx = (sx + sx) + (exy + exz)
    yy = (sy + sy) + (exy + eyz)
    zz = (sz + sz) + (exz + eyz)
    total = xx + yy + zz
    edges = exy + exz + eyz
    density = g[0] * np.float32(1 / 3) + (total - edges) * np.float32(1 / 36)
    ux2, uy2, uz2 = ux * ux, uy * uy, uz * uz
    u2 = ux2 + uy2 + uz2
    keep = 1.0 - rate
    quarter = 0.25 * keep
    base = density - u2 * sixth
    face = base + (keep * np.float32(1 / 3)) * u2 - (quarter * np.float32(1 / 3)) * total
    half_less = 0.5 - keep
    out = [None] * 19
    out[0] = base
    for first, along, u, square in ((1, xx, ux, ux2), (3, yy, uy, uy2), (5, zz, uz, uz2)):
        even = face + quarter * along + half_less * square
        out[first], out[first + 1] = even + u, even - u
    hx, hy, hz = 0.5 * ux2, 0.5 * uy2, 0.5 * uz2
    for first, ua, ub, ha, hb, q in (
        (7, ux, uy, hx, hy, qxy),
        (11, ux, uz, hx, hz, qxz),
        (15, uy, uz, hy, hz, qyz),
    ):
        cross = rate * (ua * ub) + quarter * q
        even = base + (ha + hb)
        plus, minus = even + cross, even - cross
        add, sub = ua + ub, ua - ub
        out[first], out[first + 3] = plus + add, plus - add
        out[first + 1], out[first + 2] = minus + sub, minus - sub
    return out


def roll(v, shift):
    shift = shift % LANES
    return v if shift == 0 else pltpu.roll(v, shift, 1)


def weighted(terms):
    groups = {}
    for factor, v in terms:
        if factor:
            groups.setdefault(abs(factor), []).append((factor > 0, v))
    total = None
    for factor, members in sorted(groups.items()):
        part = None
        for positive, v in members:
            if part is None:
                part = v if positive else -v
            else:
                part = part + v if positive else part - v
        part = part * np.float32(factor)
        total = part if total is None else total + part
    return total


def crossing_moments(g):
    weight = {i: (12, 2, 1)[sum(map(abs, VEL[i]))] / 36 for i in g}

    def total(factor):
        return weighted([(factor(*VEL[i], weight[i]), v) for i, v in g.items()])

    return [
        total(lambda x, y, z, w: w),
        total(lambda x, y, z, w: 3 * x * w),
        total(lambda x, y, z, w: 3 * y * w),
        total(lambda x, y, z, w: 3 * z * w),
        total(lambda x, y, z, w: x * z),
        total(lambda x, y, z, w: y * z),
        total(lambda x, y, z, w: 12 * w * (3 * z * z - x * x - y * y - z * z)),
    ]


def collide_crossing(moments, rate, members):
    density, ux, uy, uz, qxz, qyz, zz = moments
    sixth = np.float32(1 / 6)
    keep = 1.0 - rate
    quarter = 0.25 * keep
    u2 = ux * ux + uy * uy + uz * uz
    base = density - u2 * sixth
    out = []
    for i in members:
        cx, cy, cz = VEL[i]
        if cx or cy:
            u, q, sign = (ux, qxz, cx) if cx else (uy, qyz, cy)
            cross = rate * (u * uz) + quarter * q
            even = base + 0.5 * (u * u + uz * uz)
            even = even + cross if sign * cz > 0 else even - cross
            even = even + u if sign > 0 else even - u
        else:
            even = base + (keep * np.float32(1 / 3)) * u2 + quarter * zz + (0.5 - keep) * (uz * uz)
        out.append(even + uz if cz > 0 else even - uz)
    return out


def turn(v, shift):
    return roll(v, shift) if isinstance(shift, int) else pltpu.roll(v, shift & (LANES - 1), 1)


def kernel(
    n_dev,
    x_hbm,
    flags_hbm,
    near_hbm,
    rate_ref,
    out_ref,
    x_ref,
    flags_ref,
    near_ref,
    c1_ref,
    c2_ref,
    g1_ref,
    index_ref,
    absent_ref,
    halo_ref,
    send1,
    send2,
    land1,
    land2,
    in_sem,
    small_sem,
    send_sem,
    recv_sem,
):
    me = lax.axis_index("dev")
    to = (lax.min(me + 1, n_dev - 1), lax.max(me - 1, 0))
    sends = (me < n_dev - 1, me > 0)
    hears = (me > 0, me < n_dev - 1)

    def fetch(r):
        part = pl.ds(r * 4, 4)
        return pltpu.make_async_copy(x_hbm.at[:, part], x_ref.at[:, part], in_sem.at[r])

    fetch_flags = pltpu.make_async_copy(flags_hbm, flags_ref, small_sem.at[0])
    fetch_near = pltpu.make_async_copy(near_hbm, near_ref, small_sem.at[1])
    fetch_flags.start()
    fetch_near.start()
    for r in range(4):
        fetch(r).start()

    barrier = pltpu.get_barrier_semaphore()
    for side in range(2):

        @pl.when(sends[side])
        def _(side=side):
            pl.semaphore_signal(barrier, inc=1, device_id={"dev": to[side]}, device_id_type=MESH)

    lane = lax.broadcasted_iota(jnp.int32, (8, LANES), 1)
    row = lax.broadcasted_iota(jnp.int32, (8, LANES), 0)
    z = lane & 15
    z_rim = {1: z == 0, -1: z == 15}
    y_rim = {1: lane >= 112, -1: lane < 16}
    half = row >> 2

    rate = jnp.full((8, LANES), rate_ref[0], jnp.float32)
    for s in range(1, SLOTS):
        rate = jnp.where((row & 3) == s, rate_ref[s], rate)

    fetch_near.wait()
    near = near_ref[...]
    near = jnp.concatenate([near, near], axis=0)
    entry = {d: jnp.broadcast_to(near[:, k : k + 1], (8, LANES)) for k, d in enumerate(VEL[1:])}
    own = {d: (e & 3, e >= 0) for d, e in entry.items()}
    theirs = {}
    for d in VEL[1:]:
        if d[2]:
            e = entry[tuple(-c for c in d)]
            slot, there = row & 3, None
            for m in range(4):
                named = pltpu.roll(e, m, 0) if m else e
                match = named == (1 - d[2]) * 4 + (row & 3)
                slot = jnp.where(match, (row - m) & 3, slot)
                there = match if there is None else there | match
            theirs[d] = (slot, there)

    for table, first_row in ((own, 0), (theirs, 18)):
        for d, (slot, there) in table.items():
            if d[1] == 0:
                index = slot + 4 * half
            else:
                own_half = half == (1 if d[1] == -1 else 0)
                main = (d[0], 0, d[2])
                main_slot, main_there = (row & 3, row >= 0) if main == (0, 0, 0) else table[main]
                slot = jnp.where(own_half, main_slot, slot)
                there = (own_half & main_there) | (jnp.logical_not(own_half) & there)
                index = slot + 4 * (1 - half)
            index_ref[first_row + column(d)] = index
            absent_ref[first_row + column(d)] = jnp.where(there, 0.0, CLOSED)

    def look(v, d):
        k = column(d)
        return jnp.take_along_axis(v, index_ref[k], axis=0, mode="promise_in_bounds") + absent_ref[k]

    def look_across(v, d, first_row=0):
        k = first_row + column(d)
        found = jnp.take_along_axis(v, index_ref[k], axis=0, mode="promise_in_bounds")
        return jnp.where(absent_ref[k] > 0.0, CLOSED, found)

    def gathered(x, v, layer, into):
        moved = turn(v, x - layer)
        return moved if into is None else jnp.where(z == x, moved, into)

    fetch_flags.wait()
    wet = [None, None]
    for x in range(16):
        flag = (flags_ref[x] > 0).astype(jnp.float32)
        for side, layer in enumerate((15, 0)):
            wet[side] = gathered(x, flag, layer, wet[side])
    for side in range(2):
        send1[side, 5] = wet[side]
        send1[side, 6] = rate

    def value_copy(step, side, target=None):
        return pltpu.make_async_remote_copy(
            src_ref=(send1, send2)[step].at[side],
            dst_ref=(land1, land2)[step].at[side],
            send_sem=send_sem.at[step, side],
            recv_sem=recv_sem.at[step, side],
            device_id={"dev": to[side] if target is None else target},
            device_id_type=MESH,
        )

    def first(r, packed):
        fetch(r).wait()
        packed = list(packed)
        for k in range(4):
            x = 4 * r + k
            out = collide([x_ref[i, x] for i in range(19)], rate)
            fluid = flags_ref[x] > 0
            for i in range(19):
                c1_ref[i, x + 1] = jnp.where(fluid, out[i], CLOSED)
            for n, i in enumerate(UP + DOWN):
                packed[n] = gathered(x, out[i], 15 if n < 5 else 0, packed[n])
        return tuple(packed)

    packed = lax.fori_loop(0, 4, first, (jnp.zeros((8, LANES), jnp.float32),) * 10)
    for n in range(10):
        send1[n // 5, n % 5] = packed[n]

    second_core = (me & 1) == 1

    def send_first():
        pl.semaphore_wait(barrier, jnp.where(hears[0] & hears[1], 2, 1))
        early = jnp.where(second_core, 0, 1)
        for side in (early, 1 - early):

            @pl.when(((side == 0) & sends[0]) | ((side == 1) & sends[1]))
            def _(side=side):
                value_copy(0, side, jnp.where(side == 0, to[0], to[1])).start()

    def inner(c_ref, emit, between=None):
        for i in range(1, 19):
            cx, cy, cz = VEL[i]
            if cx:
                source, rim = (16, 0) if cx == 1 else (1, 17)
                c_ref[i, rim] = look(c_ref[i, source], (-cx, 0, 0))

        def settle(i, x, v):
            cx, cy, cz = VEL[i]
            v = roll(v, 16 * cy + cz)
            shut = v == CLOSED
            if cz:
                shut = shut | z_rim[cz]
            emit(i, x, jnp.where(shut, c_ref[OPP[i], x + 1], v))

        def part(r, _):
            for k in range(INNER):
                x = INNER * r + k
                emit(0, x, c_ref[0, x + 1])
                for i in range(1, 19):
                    cx, cy, cz = VEL[i]
                    v = c_ref[i, x + 1 - cx]
                    if cy:
                        v = jnp.where(y_rim[cy], look(v, (0, -cy, 0)), v)
                    settle(i, x, v)
            return 0

        steps = 16 // INNER
        if between is None:
            lax.fori_loop(0, steps, part, 0)
        else:
            lax.fori_loop(0, steps // 2, part, 0)
            between()
            lax.fori_loop(steps // 2, steps, part, 0)
        for i in range(1, 19):
            cx, cy, cz = VEL[i]
            if cx and cy:
                source, rim, x = (16, 0, 0) if cx == 1 else (1, 17, 15)
                v = jnp.where(y_rim[cy], look(c_ref[i, source], (-cx, -cy, 0)), c_ref[i, rim])
                settle(i, x, v)

    def landed(step, side):
        @pl.when(hears[side])
        def _():
            value_copy(step, side).wait_recv()

    def crossed(v, i, first_row=0):
        cx, cy, cz = VEL[i]
        face = look_across(v, (0, 0, -cz), first_row)
        if cx:
            away = roll(look_across(v, (-cx, 0, -cz), first_row), -15 * cx)
            return jnp.where(z == (0 if cx == 1 else 15), away, roll(face, cx))
        if cy:
            return roll(jnp.where(y_rim[cy], look_across(v, (0, -cy, -cz), first_row), face), 16 * cy)
        return face

    def outer(step, i, x, current):
        cz = VEL[i][2]
        side = 0 if cz == 1 else 1
        v = turn(halo_ref[step, side, (UP, DOWN)[side].index(i)], (0 if cz == 1 else 15) - x)
        return jnp.where(z_rim[cz] & (v != CLOSED), v, current)

    def keep(i, x, v):
        g1_ref[i, x] = v

    inner(c1_ref, keep, send_first)

    def send_second(side):
        g = {}
        for i in PLANE + (UP, DOWN)[side]:
            into = None
            for x in range(16):
                into = gathered(x, g1_ref[i, x], (15, 0)[side], into)
            g[i] = into
        for n, v in enumerate(crossing_moments(g)):
            send2[side, n] = v

        @pl.when(sends[side])
        def _():
            value_copy(1, side).start()

    @pl.when(second_core)
    def _():
        send_second(0)

    send_second(1)

    @pl.when(jnp.logical_not(second_core))
    def _():
        send_second(0)

    for side in range(2):
        landed(0, side)
        for p, i in enumerate((UP, DOWN)[side]):
            v = jnp.where(land1[side, 5] > 0.0, land1[side, p], CLOSED)
            halo_ref[0, side, p] = crossed(v, i)

    def second(r, _):
        for k in range(4):
            x = 4 * r + k
            g = [g1_ref[i, x] for i in range(19)]
            out = collide([outer(0, i, x, g[i]) if VEL[i][2] else g[i] for i in range(19)], rate)
            fluid = flags_ref[x] > 0
            for i in range(19):
                c2_ref[i, x + 1] = jnp.where(fluid, out[i], CLOSED)
        return 0

    lax.fori_loop(0, 4, second, 0)

    def finish(i, x, v):
        out_ref[i, x] = jnp.where(flags_ref[x] > 0, v, x_ref[i, x])

    def keep_or_finish(i, x, v):
        if VEL[i][2]:
            g1_ref[i, x] = v
        else:
            finish(i, x, v)

    inner(c2_ref, keep_or_finish)
    for side in range(2):
        theirs_out, theirs_in = (UP, DOWN) if side == 0 else (DOWN, UP)
        landed(1, side)
        g = {}
        for p, i in enumerate(theirs_in):
            v = jnp.where(send1[1 - side, 5] > 0.0, send1[1 - side, p], CLOSED)
            v = crossed(v, i, 18)
            g[i] = jnp.where(v != CLOSED, v, land1[side, theirs_out.index(OPP[i])])
        moments = [land2[side, n] + v for n, v in enumerate(crossing_moments(g))]
        out = collide_crossing(moments, land1[side, 6], theirs_out)
        for p, i in enumerate(theirs_out):
            halo_ref[1, side, p] = crossed(jnp.where(land1[side, 5] > 0.0, out[p], CLOSED), i)

    def last(r, _):
        for k in range(4):
            x = 4 * r + k
            for i in UP + DOWN:
                finish(i, x, outer(1, i, x, g1_ref[i, x]))
        return 0

    lax.fori_loop(0, 4, last, 0)
    for side in range(2):

        @pl.when(sends[side])
        def _(side=side):
            value_copy(0, side).wait_send()
            value_copy(1, side).wait_send()


def body(populations, fluid_flags, neighbours, relax_rate):
    f32, i32 = jnp.float32, jnp.int32

    def vmem(*shape, kind=f32):
        return pltpu.VMEM(shape + (8, LANES), kind)

    tiles = populations.reshape(SLOTS, 19, 16, 2, LANES).transpose(1, 2, 3, 0, 4).reshape(19, 16, 8, LANES)
    flags = fluid_flags.reshape(SLOTS, 16, 2, LANES).transpose(1, 2, 0, 3).reshape(16, 8, LANES)
    done = pl.pallas_call(
        functools.partial(kernel, lax.axis_size("dev")),
        out_shape=pltpu.VMEM((19, 16, 8, LANES), f32),
        in_specs=[
            pl.BlockSpec(memory_space=pltpu.HBM),
            pl.BlockSpec(memory_space=pltpu.HBM),
            pl.BlockSpec(memory_space=pltpu.HBM),
            pl.BlockSpec(memory_space=pltpu.SMEM),
        ],
        out_specs=pl.BlockSpec(memory_space=pltpu.VMEM),
        scratch_shapes=[
            vmem(19, 16),
            vmem(16, kind=i32),
            pltpu.VMEM((SLOTS, 18), i32),
            vmem(19, 18),
            vmem(19, 18),
            vmem(19, 16),
            vmem(36, kind=i32),
            vmem(36),
            vmem(2, 2, 5),
            vmem(2, 7),
            vmem(2, 7),
            vmem(2, 7),
            vmem(2, 7),
            pltpu.SemaphoreType.DMA((4,)),
            pltpu.SemaphoreType.DMA((2,)),
            pltpu.SemaphoreType.DMA((2, 2)),
            pltpu.SemaphoreType.DMA((2, 2)),
        ],
        compiler_params=pltpu.CompilerParams(
            collective_id=0, has_side_effects=True, vmem_limit_bytes=62 * 2**20
        ),
        name="lattice_steps",
    )(tiles, flags, neighbours, relax_rate)
    back = done.reshape(19, 16, 2, SLOTS, LANES).transpose(3, 0, 1, 2, 4)
    return back.reshape(SLOTS, 19, CELLS)


def solution(mesh):
    placed = (
        P(("group", "dev"), None, None),
        P(("group", "dev"), None),
        P(("group", "dev"), None),
        P(("group", "dev")),
    )
    return jax.shard_map(
        body, mesh=mesh, in_specs=placed, out_specs=P(("group", "dev"), None, None), check_vma=False
    )
```

```python
import functools

import jax
import jax.numpy as jnp
import numpy as np
from jax import lax
from jax.experimental import pallas as pl
from jax.experimental.pallas import tpu as pltpu
from jax.sharding import PartitionSpec as P

SLOTS = 4
CELLS = 4096
LANES = 128
INNER = 4
MESH = pl.DeviceIdType.MESH
CLOSED = np.float32(np.inf)


def velocities():
    found = [(0, 0, 0)]
    for axis in range(3):
        for sign in (1, -1):
            v = [0, 0, 0]
            v[axis] = sign
            found.append(tuple(v))
    for one, two in ((0, 1), (0, 2), (1, 2)):
        for sign_one in (1, -1):
            for sign_two in (1, -1):
                v = [0, 0, 0]
                v[one] = sign_one
                v[two] = sign_two
                found.append(tuple(v))
    return found


VEL = velocities()
OPP = [VEL.index(tuple(-c for c in v)) for v in VEL]
UP = [i for i, v in enumerate(VEL) if v[2] == 1]
DOWN = [i for i, v in enumerate(VEL) if v[2] == -1]

PLANE = [i for i, v in enumerate(VEL) if v[2] == 0]


def column(direction):
    return VEL.index(direction) - 1


def collide(g, rate):
    sx, dx = g[1] + g[2], g[1] - g[2]
    sy, dy = g[3] + g[4], g[3] - g[4]
    sz, dz = g[5] + g[6], g[5] - g[6]

    def plane(first):
        a, b = g[first] + g[first + 3], g[first + 1] + g[first + 2]
        c, d = g[first] - g[first + 3], g[first + 1] - g[first + 2]
        return a + b, a - b, c + d, c - d

    exy, qxy, x1, y1 = plane(7)
    exz, qxz, x2, z1 = plane(11)
    eyz, qyz, y2, z2 = plane(15)
    sixth = np.float32(1 / 6)
    ux = (dx + 0.5 * (x1 + x2)) * sixth
    uy = (dy + 0.5 * (y1 + y2)) * sixth
    uz = (dz + 0.5 * (z1 + z2)) * sixth
    xx = (sx + sx) + (exy + exz)
    yy = (sy + sy) + (exy + eyz)
    zz = (sz + sz) + (exz + eyz)
    total = xx + yy + zz
    edges = exy + exz + eyz
    density = g[0] * np.float32(1 / 3) + (total - edges) * np.float32(1 / 36)
    ux2, uy2, uz2 = ux * ux, uy * uy, uz * uz
    u2 = ux2 + uy2 + uz2
    keep = 1.0 - rate
    quarter = 0.25 * keep
    base = density - u2 * sixth
    face = base + (keep * np.float32(1 / 3)) * u2 - (quarter * np.float32(1 / 3)) * total
    half_less = 0.5 - keep
    out = [None] * 19
    out[0] = base
    for first, along, u, square in ((1, xx, ux, ux2), (3, yy, uy, uy2), (5, zz, uz, uz2)):
        even = face + quarter * along + half_less * square
        out[first], out[first + 1] = even + u, even - u
    hx, hy, hz = 0.5 * ux2, 0.5 * uy2, 0.5 * uz2
    for first, ua, ub, ha, hb, q in (
        (7, ux, uy, hx, hy, qxy),
        (11, ux, uz, hx, hz, qxz),
        (15, uy, uz, hy, hz, qyz),
    ):
        cross = rate * (ua * ub) + quarter * q
        even = base + (ha + hb)
        plus, minus = even + cross, even - cross
        add, sub = ua + ub, ua - ub
        out[first], out[first + 3] = plus + add, plus - add
        out[first + 1], out[first + 2] = minus + sub, minus - sub
    return out


def roll(v, shift):
    shift = shift % LANES
    return v if shift == 0 else pltpu.roll(v, shift, 1)


def weighted(terms):
    groups = {}
    for factor, v in terms:
        if factor:
            groups.setdefault(abs(factor), []).append((factor > 0, v))
    total = None
    for factor, members in sorted(groups.items()):
        part = None
        for positive, v in members:
            if part is None:
                part = v if positive else -v
            else:
                part = part + v if positive else part - v
        part = part * np.float32(factor)
        total = part if total is None else total + part
    return total


def crossing_moments(g):
    weight = {i: (12, 2, 1)[sum(map(abs, VEL[i]))] / 36 for i in g}

    def total(factor):
        return weighted([(factor(*VEL[i], weight[i]), v) for i, v in g.items()])

    return [
        total(lambda x, y, z, w: w),
        total(lambda x, y, z, w: 3 * x * w),
        total(lambda x, y, z, w: 3 * y * w),
        total(lambda x, y, z, w: 3 * z * w),
        total(lambda x, y, z, w: x * z),
        total(lambda x, y, z, w: y * z),
        total(lambda x, y, z, w: 12 * w * (3 * z * z - x * x - y * y - z * z)),
    ]


def collide_crossing(moments, rate, members):
    density, ux, uy, uz, qxz, qyz, zz = moments
    sixth = np.float32(1 / 6)
    keep = 1.0 - rate
    quarter = 0.25 * keep
    u2 = ux * ux + uy * uy + uz * uz
    base = density - u2 * sixth
    out = []
    for i in members:
        cx, cy, cz = VEL[i]
        if cx or cy:
            u, q, sign = (ux, qxz, cx) if cx else (uy, qyz, cy)
            cross = rate * (u * uz) + quarter * q
            even = base + 0.5 * (u * u + uz * uz)
            even = even + cross if sign * cz > 0 else even - cross
            even = even + u if sign > 0 else even - u
        else:
            even = base + (keep * np.float32(1 / 3)) * u2 + quarter * zz + (0.5 - keep) * (uz * uz)
        out.append(even + uz if cz > 0 else even - uz)
    return out


def turn(v, shift):
    return roll(v, shift) if isinstance(shift, int) else pltpu.roll(v, shift & (LANES - 1), 1)


def kernel(
    n_dev,
    x_hbm,
    flags_hbm,
    near_hbm,
    rate_ref,
    out_ref,
    late_ref,
    x_ref,
    flags_ref,
    near_ref,
    c1_ref,
    c2_ref,
    g1_ref,
    index_ref,
    absent_ref,
    halo_ref,
    send1,
    send2,
    land1,
    land2,
    in_sem,
    small_sem,
    send_sem,
    recv_sem,
):
    me = lax.axis_index("dev")
    to = (lax.min(me + 1, n_dev - 1), lax.max(me - 1, 0))
    sends = (me < n_dev - 1, me > 0)
    hears = (me > 0, me < n_dev - 1)

    def fetch(r):
        part = pl.ds(r * 4, 4)
        return pltpu.make_async_copy(x_hbm.at[:, part], x_ref.at[:, part], in_sem.at[r])

    fetch_flags = pltpu.make_async_copy(flags_hbm, flags_ref, small_sem.at[0])
    fetch_near = pltpu.make_async_copy(near_hbm, near_ref, small_sem.at[1])
    fetch_flags.start()
    fetch_near.start()
    for r in range(4):
        fetch(r).start()

    barrier = pltpu.get_barrier_semaphore()
    for side in range(2):

        @pl.when(sends[side])
        def _(side=side):
            pl.semaphore_signal(barrier, inc=1, device_id={"dev": to[side]}, device_id_type=MESH)

    lane = lax.broadcasted_iota(jnp.int32, (8, LANES), 1)
    row = lax.broadcasted_iota(jnp.int32, (8, LANES), 0)
    z = lane & 15
    z_rim = {1: z == 0, -1: z == 15}
    y_rim = {1: lane >= 112, -1: lane < 16}
    half = row >> 2

    rate = jnp.full((8, LANES), rate_ref[0], jnp.float32)
    for s in range(1, SLOTS):
        rate = jnp.where((row & 3) == s, rate_ref[s], rate)

    fetch_near.wait()
    near = near_ref[...]
    near = jnp.concatenate([near, near], axis=0)
    entry = {d: jnp.broadcast_to(near[:, k : k + 1], (8, LANES)) for k, d in enumerate(VEL[1:])}
    own = {d: (e & 3, e >= 0) for d, e in entry.items()}
    theirs = {}
    for d in VEL[1:]:
        if d[2]:
            e = entry[tuple(-c for c in d)]
            slot, there = row & 3, None
            for m in range(4):
                named = pltpu.roll(e, m, 0) if m else e
                match = named == (1 - d[2]) * 4 + (row & 3)
                slot = jnp.where(match, (row - m) & 3, slot)
                there = match if there is None else there | match
            theirs[d] = (slot, there)

    for table, first_row in ((own, 0), (theirs, 18)):
        for d, (slot, there) in table.items():
            if d[1] == 0:
                index = slot + 4 * half
            else:
                own_half = half == (1 if d[1] == -1 else 0)
                main = (d[0], 0, d[2])
                main_slot, main_there = (row & 3, row >= 0) if main == (0, 0, 0) else table[main]
                slot = jnp.where(own_half, main_slot, slot)
                there = (own_half & main_there) | (jnp.logical_not(own_half) & there)
                index = slot + 4 * (1 - half)
            index_ref[first_row + column(d)] = index
            absent_ref[first_row + column(d)] = jnp.where(there, 0.0, CLOSED)

    def look(v, d):
        k = column(d)
        return jnp.take_along_axis(v, index_ref[k], axis=0, mode="promise_in_bounds") + absent_ref[k]

    def look_across(v, d, first_row=0):
        k = first_row + column(d)
        found = jnp.take_along_axis(v, index_ref[k], axis=0, mode="promise_in_bounds")
        return jnp.where(absent_ref[k] > 0.0, CLOSED, found)

    def gathered(x, v, layer, into):
        moved = turn(v, x - layer)
        return moved if into is None else jnp.where(z == x, moved, into)

    fetch_flags.wait()
    wet = [None, None]
    for x in range(16):
        flag = (flags_ref[x] > 0).astype(jnp.float32)
        for side, layer in enumerate((15, 0)):
            wet[side] = gathered(x, flag, layer, wet[side])
    for side in range(2):
        send1[side, 5] = wet[side]
        send1[side, 6] = rate

    def value_copy(step, side, target=None):
        return pltpu.make_async_remote_copy(
            src_ref=(send1, send2)[step].at[side],
            dst_ref=(land1, land2)[step].at[side],
            send_sem=send_sem.at[step, side],
            recv_sem=recv_sem.at[step, side],
            device_id={"dev": to[side] if target is None else target},
            device_id_type=MESH,
        )

    def first(r, packed):
        fetch(r).wait()
        packed = list(packed)
        for k in range(4):
            x = 4 * r + k
            out = collide([x_ref[i, x] for i in range(19)], rate)
            fluid = flags_ref[x] > 0
            for i in range(19):
                c1_ref[i, x + 1] = jnp.where(fluid, out[i], CLOSED)
            for n, i in enumerate(UP + DOWN):
                packed[n] = gathered(x, out[i], 15 if n < 5 else 0, packed[n])
        return tuple(packed)

    packed = lax.fori_loop(0, 4, first, (jnp.zeros((8, LANES), jnp.float32),) * 10)
    for n in range(10):
        send1[n // 5, n % 5] = packed[n]

    second_core = (me & 1) == 1

    def send_first():
        pl.semaphore_wait(barrier, jnp.where(hears[0] & hears[1], 2, 1))
        early = jnp.where(second_core, 0, 1)
        for side in (early, 1 - early):

            @pl.when(((side == 0) & sends[0]) | ((side == 1) & sends[1]))
            def _(side=side):
                value_copy(0, side, jnp.where(side == 0, to[0], to[1])).start()

    def inner(c_ref, emit):
        for i in range(1, 19):
            cx, cy, cz = VEL[i]
            if cx:
                source, rim = (16, 0) if cx == 1 else (1, 17)
                c_ref[i, rim] = look(c_ref[i, source], (-cx, 0, 0))

        def settle(i, x, v):
            cx, cy, cz = VEL[i]
            v = roll(v, 16 * cy + cz)
            shut = v == CLOSED
            if cz:
                shut = shut | z_rim[cz]
            emit(i, x, jnp.where(shut, c_ref[OPP[i], x + 1], v))

        def part(r, _):
            for k in range(INNER):
                x = INNER * r + k
                emit(0, x, c_ref[0, x + 1])
                for i in range(1, 19):
                    cx, cy, cz = VEL[i]
                    v = c_ref[i, x + 1 - cx]
                    if cy:
                        v = jnp.where(y_rim[cy], look(v, (0, -cy, 0)), v)
                    settle(i, x, v)
            return 0

        lax.fori_loop(0, 16 // INNER, part, 0)
        for i in range(1, 19):
            cx, cy, cz = VEL[i]
            if cx and cy:
                source, rim, x = (16, 0, 0) if cx == 1 else (1, 17, 15)
                v = jnp.where(y_rim[cy], look(c_ref[i, source], (-cx, -cy, 0)), c_ref[i, rim])
                settle(i, x, v)

    def landed(step, side):
        @pl.when(hears[side])
        def _():
            value_copy(step, side).wait_recv()

    def crossed(v, i, first_row=0):
        cx, cy, cz = VEL[i]
        face = look_across(v, (0, 0, -cz), first_row)
        if cx:
            away = roll(look_across(v, (-cx, 0, -cz), first_row), -15 * cx)
            return jnp.where(z == (0 if cx == 1 else 15), away, roll(face, cx))
        if cy:
            return roll(jnp.where(y_rim[cy], look_across(v, (0, -cy, -cz), first_row), face), 16 * cy)
        return face

    def outer(i, x, current):
        cz = VEL[i][2]
        side = 0 if cz == 1 else 1
        v = turn(halo_ref[side, (UP, DOWN)[side].index(i)], (0 if cz == 1 else 15) - x)
        return jnp.where(z_rim[cz] & (v != CLOSED), v, current)

    def keep(i, x, v):
        g1_ref[i, x] = v

    send_first()
    inner(c1_ref, keep)

    def send_second(side):
        g = {}
        for i in PLANE + (UP, DOWN)[side]:
            into = None
            for x in range(16):
                into = gathered(x, g1_ref[i, x], (15, 0)[side], into)
            g[i] = into
        for n, v in enumerate(crossing_moments(g)):
            send2[side, n] = v

        @pl.when(sends[side])
        def _():
            value_copy(1, side).start()

    @pl.when(second_core)
    def _():
        send_second(0)

    send_second(1)

    @pl.when(jnp.logical_not(second_core))
    def _():
        send_second(0)

    for side in range(2):
        landed(0, side)
        for p, i in enumerate((UP, DOWN)[side]):
            v = jnp.where(land1[side, 5] > 0.0, land1[side, p], CLOSED)
            halo_ref[side, p] = crossed(v, i)

    def second(r, _):
        for k in range(4):
            x = 4 * r + k
            g = [g1_ref[i, x] for i in range(19)]
            out = collide([outer(i, x, g[i]) if VEL[i][2] else g[i] for i in range(19)], rate)
            fluid = flags_ref[x] > 0
            for i in range(19):
                c2_ref[i, x + 1] = jnp.where(fluid, out[i], CLOSED)
        return 0

    lax.fori_loop(0, 4, second, 0)

    def finish(i, x, v):
        out_ref[i, x] = jnp.where(flags_ref[x] > 0, v, x_ref[i, x])

    inner(c2_ref, finish)

    for side in range(2):
        theirs_out, theirs_in = (UP, DOWN) if side == 0 else (DOWN, UP)
        landed(1, side)
        g = {}
        for p, i in enumerate(theirs_in):
            v = jnp.where(send1[1 - side, 5] > 0.0, send1[1 - side, p], CLOSED)
            v = crossed(v, i, 18)
            g[i] = jnp.where(v != CLOSED, v, land1[side, theirs_out.index(OPP[i])])
        moments = [land2[side, n] + v for n, v in enumerate(crossing_moments(g))]
        out = collide_crossing(moments, land1[side, 6], theirs_out)
        for p, i in enumerate(theirs_out):
            v = crossed(jnp.where(land1[side, 5] > 0.0, out[p], CLOSED), i)
            late_ref[side, p] = jnp.where(send1[1 - side, 5] > 0.0, v, CLOSED)

    for side in range(2):

        @pl.when(sends[side])
        def _(side=side):
            value_copy(0, side).wait_send()
            value_copy(1, side).wait_send()


def finish_kernel(held_ref, late_ref, out_hbm, done_ref, sem):
    def write(i):
        source = done_ref.at[(UP + DOWN).index(i)] if VEL[i][2] else held_ref.at[i]
        return pltpu.make_async_copy(source, out_hbm.at[i], sem.at[i])

    for i in PLANE:
        write(i).start()
    z = lax.broadcasted_iota(jnp.int32, (8, LANES), 1) & 15
    for n, i in enumerate(UP + DOWN):
        rim = 0 if n < 5 else 15
        late = late_ref[n // 5, n % 5]
        for x in range(16):
            v = roll(late, rim - x)
            done_ref[n, x] = jnp.where((z == rim) & (v != CLOSED), v, held_ref[i, x])
        write(i).start()
    for i in range(19):
        write(i).wait()


def body(populations, fluid_flags, neighbours, relax_rate):
    f32, i32 = jnp.float32, jnp.int32

    def vmem(*shape, kind=f32):
        return pltpu.VMEM(shape + (8, LANES), kind)

    tiles = populations.reshape(SLOTS, 19, 16, 2, LANES).transpose(1, 2, 3, 0, 4).reshape(19, 16, 8, LANES)
    flags = fluid_flags.reshape(SLOTS, 16, 2, LANES).transpose(1, 2, 0, 3).reshape(16, 8, LANES)
    held, late = pl.pallas_call(
        functools.partial(kernel, lax.axis_size("dev")),
        out_shape=(pltpu.VMEM((19, 16, 8, LANES), f32), pltpu.VMEM((2, 5, 8, LANES), f32)),
        in_specs=[
            pl.BlockSpec(memory_space=pltpu.HBM),
            pl.BlockSpec(memory_space=pltpu.HBM),
            pl.BlockSpec(memory_space=pltpu.HBM),
            pl.BlockSpec(memory_space=pltpu.SMEM),
        ],
        out_specs=(pl.BlockSpec(memory_space=pltpu.VMEM),) * 2,
        scratch_shapes=[
            vmem(19, 16),
            vmem(16, kind=i32),
            pltpu.VMEM((SLOTS, 18), i32),
            vmem(19, 18),
            vmem(19, 18),
            vmem(19, 16),
            vmem(36, kind=i32),
            vmem(36),
            vmem(2, 5),
            vmem(2, 7),
            vmem(2, 7),
            vmem(2, 7),
            vmem(2, 7),
            pltpu.SemaphoreType.DMA((4,)),
            pltpu.SemaphoreType.DMA((2,)),
            pltpu.SemaphoreType.DMA((2, 2)),
            pltpu.SemaphoreType.DMA((2, 2)),
        ],
        compiler_params=pltpu.CompilerParams(
            collective_id=0, has_side_effects=True, vmem_limit_bytes=62 * 2**20
        ),
        name="lattice_steps",
    )(tiles, flags, neighbours, relax_rate)
    done = pl.pallas_call(
        finish_kernel,
        out_shape=jax.ShapeDtypeStruct((19, 16, 8, LANES), f32),
        in_specs=[pl.BlockSpec(memory_space=pltpu.VMEM)] * 2,
        out_specs=pl.BlockSpec(memory_space=pltpu.HBM),
        scratch_shapes=[vmem(10, 16), pltpu.SemaphoreType.DMA((19,))],
        compiler_params=pltpu.CompilerParams(vmem_limit_bytes=16 * 2**20),
        name="finish",
    )(held, late)
    back = done.reshape(19, 16, 2, SLOTS, LANES).transpose(3, 0, 1, 2, 4)
    return back.reshape(SLOTS, 19, CELLS)


def solution(mesh):
    placed = (
        P(("group", "dev"), None, None),
        P(("group", "dev"), None),
        P(("group", "dev"), None),
        P(("group", "dev")),
    )
    return jax.shard_map(
        body, mesh=mesh, in_specs=placed, out_specs=P(("group", "dev"), None, None), check_vma=False
    )
```

```python
import functools

import jax
import jax.numpy as jnp
import numpy as np
from jax import lax
from jax.experimental import pallas as pl
from jax.experimental.pallas import tpu as pltpu
from jax.sharding import PartitionSpec as P

SLOTS = 4
CELLS = 4096
LANES = 128
INNER = 4
MESH = pl.DeviceIdType.MESH
CLOSED = np.float32(np.inf)


def velocities():
    found = [(0, 0, 0)]
    for axis in range(3):
        for sign in (1, -1):
            v = [0, 0, 0]
            v[axis] = sign
            found.append(tuple(v))
    for one, two in ((0, 1), (0, 2), (1, 2)):
        for sign_one in (1, -1):
            for sign_two in (1, -1):
                v = [0, 0, 0]
                v[one] = sign_one
                v[two] = sign_two
                found.append(tuple(v))
    return found


VEL = velocities()
OPP = [VEL.index(tuple(-c for c in v)) for v in VEL]
UP = [i for i, v in enumerate(VEL) if v[2] == 1]
DOWN = [i for i, v in enumerate(VEL) if v[2] == -1]

PLANE = [i for i, v in enumerate(VEL) if v[2] == 0]


def column(direction):
    return VEL.index(direction) - 1


def collide(g, rate):
    sx, dx = g[1] + g[2], g[1] - g[2]
    sy, dy = g[3] + g[4], g[3] - g[4]
    sz, dz = g[5] + g[6], g[5] - g[6]

    def plane(first):
        a, b = g[first] + g[first + 3], g[first + 1] + g[first + 2]
        c, d = g[first] - g[first + 3], g[first + 1] - g[first + 2]
        return a + b, a - b, c + d, c - d

    exy, qxy, x1, y1 = plane(7)
    exz, qxz, x2, z1 = plane(11)
    eyz, qyz, y2, z2 = plane(15)
    sixth = np.float32(1 / 6)
    ux = (dx + 0.5 * (x1 + x2)) * sixth
    uy = (dy + 0.5 * (y1 + y2)) * sixth
    uz = (dz + 0.5 * (z1 + z2)) * sixth
    xx = (sx + sx) + (exy + exz)
    yy = (sy + sy) + (exy + eyz)
    zz = (sz + sz) + (exz + eyz)
    total = xx + yy + zz
    edges = exy + exz + eyz
    density = g[0] * np.float32(1 / 3) + (total - edges) * np.float32(1 / 36)
    ux2, uy2, uz2 = ux * ux, uy * uy, uz * uz
    u2 = ux2 + uy2 + uz2
    keep = 1.0 - rate
    quarter = 0.25 * keep
    base = density - u2 * sixth
    face = base + (keep * np.float32(1 / 3)) * u2 - (quarter * np.float32(1 / 3)) * total
    half_less = 0.5 - keep
    out = [None] * 19
    out[0] = base
    for first, along, u, square in ((1, xx, ux, ux2), (3, yy, uy, uy2), (5, zz, uz, uz2)):
        even = face + quarter * along + half_less * square
        out[first], out[first + 1] = even + u, even - u
    hx, hy, hz = 0.5 * ux2, 0.5 * uy2, 0.5 * uz2
    for first, ua, ub, ha, hb, q in (
        (7, ux, uy, hx, hy, qxy),
        (11, ux, uz, hx, hz, qxz),
        (15, uy, uz, hy, hz, qyz),
    ):
        cross = rate * (ua * ub) + quarter * q
        even = base + (ha + hb)
        plus, minus = even + cross, even - cross
        add, sub = ua + ub, ua - ub
        out[first], out[first + 3] = plus + add, plus - add
        out[first + 1], out[first + 2] = minus + sub, minus - sub
    return out


def roll(v, shift):
    shift = shift % LANES
    return v if shift == 0 else pltpu.roll(v, shift, 1)


def weighted(terms):
    groups = {}
    for factor, v in terms:
        if factor:
            groups.setdefault(abs(factor), []).append((factor > 0, v))
    total = None
    for factor, members in sorted(groups.items()):
        part = None
        for positive, v in members:
            if part is None:
                part = v if positive else -v
            else:
                part = part + v if positive else part - v
        part = part * np.float32(factor)
        total = part if total is None else total + part
    return total


def crossing_moments(g):
    weight = {i: (12, 2, 1)[sum(map(abs, VEL[i]))] / 36 for i in g}

    def total(factor):
        return weighted([(factor(*VEL[i], weight[i]), v) for i, v in g.items()])

    return [
        total(lambda x, y, z, w: w),
        total(lambda x, y, z, w: 3 * x * w),
        total(lambda x, y, z, w: 3 * y * w),
        total(lambda x, y, z, w: 3 * z * w),
        total(lambda x, y, z, w: x * z),
        total(lambda x, y, z, w: y * z),
        total(lambda x, y, z, w: 12 * w * (3 * z * z - x * x - y * y - z * z)),
    ]


def collide_crossing(moments, rate, members):
    density, ux, uy, uz, qxz, qyz, zz = moments
    sixth = np.float32(1 / 6)
    keep = 1.0 - rate
    quarter = 0.25 * keep
    u2 = ux * ux + uy * uy + uz * uz
    base = density - u2 * sixth
    out = []
    for i in members:
        cx, cy, cz = VEL[i]
        if cx or cy:
            u, q, sign = (ux, qxz, cx) if cx else (uy, qyz, cy)
            cross = rate * (u * uz) + quarter * q
            even = base + 0.5 * (u * u + uz * uz)
            even = even + cross if sign * cz > 0 else even - cross
            even = even + u if sign > 0 else even - u
        else:
            even = base + (keep * np.float32(1 / 3)) * u2 + quarter * zz + (0.5 - keep) * (uz * uz)
        out.append(even + uz if cz > 0 else even - uz)
    return out


def turn(v, shift):
    return roll(v, shift) if isinstance(shift, int) else pltpu.roll(v, shift & (LANES - 1), 1)


def kernel(
    n_dev,
    x_hbm,
    flags_hbm,
    near_hbm,
    rate_ref,
    out_ref,
    late_ref,
    x_ref,
    flags_ref,
    near_ref,
    c1_ref,
    c2_ref,
    g1_ref,
    index_ref,
    absent_ref,
    layer_ref,
    wet_ref,
    send1,
    send2,
    land1,
    land2,
    in_sem,
    small_sem,
    send_sem,
    recv_sem,
):
    me = lax.axis_index("dev")
    to = (lax.min(me + 1, n_dev - 1), lax.max(me - 1, 0))
    sends = (me < n_dev - 1, me > 0)
    hears = (me > 0, me < n_dev - 1)

    def fetch(r):
        part = pl.ds(r * 4, 4)
        return pltpu.make_async_copy(x_hbm.at[:, part], x_ref.at[:, part], in_sem.at[r])

    fetch_flags = pltpu.make_async_copy(flags_hbm, flags_ref, small_sem.at[0])
    fetch_near = pltpu.make_async_copy(near_hbm, near_ref, small_sem.at[1])
    fetch_flags.start()
    fetch_near.start()
    for r in range(4):
        fetch(r).start()

    barrier = pltpu.get_barrier_semaphore()
    for side in range(2):

        @pl.when(sends[side])
        def _(side=side):
            pl.semaphore_signal(barrier, inc=1, device_id={"dev": to[side]}, device_id_type=MESH)

    lane = lax.broadcasted_iota(jnp.int32, (8, LANES), 1)
    row = lax.broadcasted_iota(jnp.int32, (8, LANES), 0)
    z = lane & 15
    z_rim = {1: z == 0, -1: z == 15}
    y_rim = {1: lane >= 112, -1: lane < 16}
    half = row >> 2

    rate = jnp.full((8, LANES), rate_ref[0], jnp.float32)
    for s in range(1, SLOTS):
        rate = jnp.where((row & 3) == s, rate_ref[s], rate)

    fetch_near.wait()
    near = near_ref[...]
    near = jnp.concatenate([near, near], axis=0)
    entry = {d: jnp.broadcast_to(near[:, k : k + 1], (8, LANES)) for k, d in enumerate(VEL[1:])}
    own = {d: (e & 3, e >= 0) for d, e in entry.items()}
    theirs = {}
    for d in VEL[1:]:
        if d[2]:
            e = entry[tuple(-c for c in d)]
            slot, there = row & 3, None
            for m in range(4):
                named = pltpu.roll(e, m, 0) if m else e
                match = named == (1 - d[2]) * 4 + (row & 3)
                slot = jnp.where(match, (row - m) & 3, slot)
                there = match if there is None else there | match
            theirs[d] = (slot, there)

    for table, first_row in ((own, 0), (theirs, 18)):
        for d, (slot, there) in table.items():
            if d[1] == 0:
                index = slot + 4 * half
            else:
                own_half = half == (1 if d[1] == -1 else 0)
                main = (d[0], 0, d[2])
                main_slot, main_there = (row & 3, row >= 0) if main == (0, 0, 0) else table[main]
                slot = jnp.where(own_half, main_slot, slot)
                there = (own_half & main_there) | (jnp.logical_not(own_half) & there)
                index = slot + 4 * (1 - half)
            index_ref[first_row + column(d)] = index
            absent_ref[first_row + column(d)] = jnp.where(there, 0.0, CLOSED)

    def look(v, d):
        k = column(d)
        return jnp.take_along_axis(v, index_ref[k], axis=0, mode="promise_in_bounds") + absent_ref[k]

    def look_across(v, d, first_row=0):
        k = first_row + column(d)
        found = jnp.take_along_axis(v, index_ref[k], axis=0, mode="promise_in_bounds")
        return jnp.where(absent_ref[k] > 0.0, CLOSED, found)

    def gathered(x, v, layer, into):
        moved = turn(v, x - layer)
        return moved if into is None else jnp.where(z == x, moved, into)

    fetch_flags.wait()
    wet = [None] * 4
    for x in range(16):
        flag = (flags_ref[x] > 0).astype(jnp.float32)
        for side, layer in enumerate((15, 0, 14, 1)):
            wet[side] = gathered(x, flag, layer, wet[side])
    for side in range(2):
        send1[side, 5] = wet[side]
        send1[side, 6] = rate
        wet_ref[side] = wet[2 + side]

    def value_copy(step, side, target=None):
        return pltpu.make_async_remote_copy(
            src_ref=(send1, send2)[step].at[side],
            dst_ref=(land1, land2)[step].at[side],
            send_sem=send_sem.at[step, side],
            recv_sem=recv_sem.at[step, side],
            device_id={"dev": to[side] if target is None else target},
            device_id_type=MESH,
        )

    def first(r, packed):
        fetch(r).wait()
        packed = list(packed)
        for k in range(4):
            x = 4 * r + k
            out = collide([x_ref[i, x] for i in range(19)], rate)
            fluid = flags_ref[x] > 0
            for i in range(19):
                c1_ref[i, x + 1] = jnp.where(fluid, out[i], CLOSED)
            for n, i in enumerate(UP + DOWN):
                packed[n] = gathered(x, out[i], 15 if n < 5 else 0, packed[n])
        return tuple(packed)

    packed = lax.fori_loop(0, 4, first, (jnp.zeros((8, LANES), jnp.float32),) * 10)
    for n in range(10):
        send1[n // 5, n % 5] = packed[n]

    second_core = (me & 1) == 1

    def send_first():
        pl.semaphore_wait(barrier, jnp.where(hears[0] & hears[1], 2, 1))
        early = jnp.where(second_core, 0, 1)
        for side in (early, 1 - early):

            @pl.when(((side == 0) & sends[0]) | ((side == 1) & sends[1]))
            def _(side=side):
                value_copy(0, side, jnp.where(side == 0, to[0], to[1])).start()

    def inner(c_ref, emit):
        for i in range(1, 19):
            cx, cy, cz = VEL[i]
            if cx:
                source, rim = (16, 0) if cx == 1 else (1, 17)
                c_ref[i, rim] = look(c_ref[i, source], (-cx, 0, 0))

        def settle(i, x, v):
            cx, cy, cz = VEL[i]
            v = roll(v, 16 * cy + cz)
            shut = v == CLOSED
            if cz:
                shut = shut | z_rim[cz]
            emit(i, x, jnp.where(shut, c_ref[OPP[i], x + 1], v))

        def part(r, _):
            for k in range(INNER):
                x = INNER * r + k
                emit(0, x, c_ref[0, x + 1])
                for i in range(1, 19):
                    cx, cy, cz = VEL[i]
                    v = c_ref[i, x + 1 - cx]
                    if cy:
                        v = jnp.where(y_rim[cy], look(v, (0, -cy, 0)), v)
                    settle(i, x, v)
            return 0

        lax.fori_loop(0, 16 // INNER, part, 0)
        for i in range(1, 19):
            cx, cy, cz = VEL[i]
            if cx and cy:
                source, rim, x = (16, 0, 0) if cx == 1 else (1, 17, 15)
                v = jnp.where(y_rim[cy], look(c_ref[i, source], (-cx, -cy, 0)), c_ref[i, rim])
                settle(i, x, v)

    def landed(step, side):
        @pl.when(hears[side])
        def _():
            value_copy(step, side).wait_recv()

    def crossed(v, i, first_row=0):
        cx, cy, cz = VEL[i]
        face = look_across(v, (0, 0, -cz), first_row)
        if cx:
            away = roll(look_across(v, (-cx, 0, -cz), first_row), -15 * cx)
            return jnp.where(z == (0 if cx == 1 else 15), away, roll(face, cx))
        if cy:
            return roll(jnp.where(y_rim[cy], look_across(v, (0, -cy, -cz), first_row), face), 16 * cy)
        return face

    def keep(i, x, v):
        g1_ref[i, x] = v

    send_first()
    inner(c1_ref, keep)

    def send_second(side):
        g = {}
        for i in PLANE + (UP, DOWN)[side]:
            into = None
            for x in range(16):
                into = gathered(x, g1_ref[i, x], (15, 0)[side], into)
            g[i] = into
            layer_ref[side, i] = into
        for n, v in enumerate(crossing_moments(g)):
            send2[side, n] = v

        @pl.when(sends[side])
        def _():
            value_copy(1, side).start()

    @pl.when(second_core)
    def _():
        send_second(0)

    send_second(1)

    @pl.when(jnp.logical_not(second_core))
    def _():
        send_second(0)

    def second(r, _):
        for k in range(4):
            x = 4 * r + k
            g = [g1_ref[i, x] for i in range(19)]
            out = collide(g, rate)
            fluid = flags_ref[x] > 0
            for i in range(19):
                c2_ref[i, x + 1] = jnp.where(fluid, out[i], CLOSED)
        return 0

    lax.fori_loop(0, 4, second, 0)

    def finish(i, x, v):
        out_ref[i, x] = jnp.where(flags_ref[x] > 0, v, x_ref[i, x])

    inner(c2_ref, finish)

    def in_plane(v, i):
        cx, cy, _ = VEL[i]
        here = jnp.where(y_rim[cy], look_across(v, (0, -cy, 0)), v) if cy else v
        here = roll(here, 16 * cy + cx)
        if cx:
            away = look_across(v, (-cx, 0, 0))
            if cy:
                away = jnp.where(y_rim[cy], look_across(v, (-cx, -cy, 0)), away)
            here = jnp.where(z == (0 if cx == 1 else 15), roll(away, 16 * cy - 15 * cx), here)
        return here

    for side in range(2):
        outs, ins = (UP, DOWN) if side == 0 else (DOWN, UP)
        arriving = 1 - side
        landed(0, arriving)
        g = {i: layer_ref[side, i] for i in PLANE + outs}
        for p, i in enumerate(ins):
            v = crossed(jnp.where(land1[arriving, 5] > 0.0, land1[arriving, p], CLOSED), i)
            g[i] = jnp.where(v != CLOSED, v, send1[side, outs.index(OPP[i])])
        fluid, below_fluid = send1[side, 5] > 0.0, wet_ref[side] > 0.0
        c = [jnp.where(fluid, v, CLOSED) for v in collide([g[i] for i in range(19)], rate)]
        late_ref[side, 0] = c[0]
        for i in PLANE[1:]:
            v = in_plane(c[i], i)
            late_ref[side, i] = jnp.where(fluid, jnp.where(v != CLOSED, v, c[OPP[i]]), CLOSED)
        for i in outs:
            v = in_plane(jnp.where(below_fluid, 0.0, CLOSED), i)
            late_ref[side, i] = jnp.where(v == CLOSED, c[OPP[i]], CLOSED)
        for p, i in enumerate(ins):
            late_ref[side, i] = c[OPP[i]]
            late_ref[side, 19 + p] = jnp.where(below_fluid, in_plane(c[i], i), CLOSED)

    for side in range(2):
        theirs_out, theirs_in = (UP, DOWN) if side == 0 else (DOWN, UP)
        landed(1, side)
        g = {}
        for p, i in enumerate(theirs_in):
            v = jnp.where(send1[1 - side, 5] > 0.0, send1[1 - side, p], CLOSED)
            v = crossed(v, i, 18)
            g[i] = jnp.where(v != CLOSED, v, land1[side, theirs_out.index(OPP[i])])
        moments = [land2[side, n] + v for n, v in enumerate(crossing_moments(g))]
        out = collide_crossing(moments, land1[side, 6], theirs_out)
        for p, i in enumerate(theirs_out):
            v = crossed(jnp.where(land1[side, 5] > 0.0, out[p], CLOSED), i)
            late_ref[1 - side, i] = jnp.where((send1[1 - side, 5] > 0.0) & (v != CLOSED), v, late_ref[1 - side, i])

    for side in range(2):

        @pl.when(sends[side])
        def _(side=side):
            value_copy(0, side).wait_send()
            value_copy(1, side).wait_send()


def finish_kernel(held_ref, late_ref, out_hbm, done_ref, sem):
    z = lax.broadcasted_iota(jnp.int32, (8, LANES), 1) & 15
    copies = []
    for i in range(19):
        parts = [(15, late_ref[0, i]), (0, late_ref[1, i])]
        if i in DOWN:
            parts.append((14, late_ref[0, 19 + DOWN.index(i)]))
        if i in UP:
            parts.append((1, late_ref[1, 19 + UP.index(i)]))
        for x in range(16):
            v = held_ref[i, x]
            for at, late in parts:
                moved = roll(late, at - x)
                v = jnp.where((z == at) & (moved != CLOSED), moved, v)
            done_ref[i, x] = v
        copies.append(pltpu.make_async_copy(done_ref.at[i], out_hbm.at[i], sem.at[i]))
        copies[-1].start()
    for copy in copies:
        copy.wait()


def body(populations, fluid_flags, neighbours, relax_rate):
    f32, i32 = jnp.float32, jnp.int32

    def vmem(*shape, kind=f32):
        return pltpu.VMEM(shape + (8, LANES), kind)

    tiles = populations.reshape(SLOTS, 19, 16, 2, LANES).transpose(1, 2, 3, 0, 4).reshape(19, 16, 8, LANES)
    flags = fluid_flags.reshape(SLOTS, 16, 2, LANES).transpose(1, 2, 0, 3).reshape(16, 8, LANES)
    held, late = pl.pallas_call(
        functools.partial(kernel, lax.axis_size("dev")),
        out_shape=(pltpu.VMEM((19, 16, 8, LANES), f32), pltpu.VMEM((2, 24, 8, LANES), f32)),
        in_specs=[
            pl.BlockSpec(memory_space=pltpu.HBM),
            pl.BlockSpec(memory_space=pltpu.HBM),
            pl.BlockSpec(memory_space=pltpu.HBM),
            pl.BlockSpec(memory_space=pltpu.SMEM),
        ],
        out_specs=(pl.BlockSpec(memory_space=pltpu.VMEM),) * 2,
        scratch_shapes=[
            vmem(19, 16),
            vmem(16, kind=i32),
            pltpu.VMEM((SLOTS, 18), i32),
            vmem(19, 18),
            vmem(19, 18),
            vmem(19, 16),
            vmem(36, kind=i32),
            vmem(36),
            vmem(2, 19),
            vmem(2),
            vmem(2, 7),
            vmem(2, 7),
            vmem(2, 7),
            vmem(2, 7),
            pltpu.SemaphoreType.DMA((4,)),
            pltpu.SemaphoreType.DMA((2,)),
            pltpu.SemaphoreType.DMA((2, 2)),
            pltpu.SemaphoreType.DMA((2, 2)),
        ],
        compiler_params=pltpu.CompilerParams(
            collective_id=0, has_side_effects=True, vmem_limit_bytes=62 * 2**20
        ),
        name="lattice_steps",
    )(tiles, flags, neighbours, relax_rate)
    done = pl.pallas_call(
        finish_kernel,
        out_shape=jax.ShapeDtypeStruct((19, 16, 8, LANES), f32),
        in_specs=[pl.BlockSpec(memory_space=pltpu.VMEM)] * 2,
        out_specs=pl.BlockSpec(memory_space=pltpu.HBM),
        scratch_shapes=[vmem(19, 16), pltpu.SemaphoreType.DMA((19,))],
        compiler_params=pltpu.CompilerParams(vmem_limit_bytes=16 * 2**20),
        name="finish",
    )(held, late)
    back = done.reshape(19, 16, 2, SLOTS, LANES).transpose(3, 0, 1, 2, 4)
    return back.reshape(SLOTS, 19, CELLS)


def solution(mesh):
    placed = (
        P(("group", "dev"), None, None),
        P(("group", "dev"), None),
        P(("group", "dev"), None),
        P(("group", "dev")),
    )
    return jax.shard_map(
        body, mesh=mesh, in_specs=placed, out_specs=P(("group", "dev"), None, None), check_vma=False
    )
```
